256 devices in a mesh: ell: 32 (over y, x, core), rad: 8 (over z).
Axes of the slice: x: 4, y: 4, z: 8, core: 2. Of those that a mesh axis runs over, the one named last changes fastest.
Arguments:
- coefficients: bfloat16 [2, 256, 768, 1537], P(None, 'rad', 'ell'), may hold values from -0.14941406 to 0.14941406
- legendre: bfloat16 [32, 768, 1537], P(None, 'ell'), may hold values from -0.15625 to 0.15625
- bessel: bfloat16 [2, 32, 256, 1536], P(None, None, 'rad', 'ell'), may hold values from -0.375 to 0.375
- mode_counts: int32 [1536], replicated, may hold values from 1 to 256, as said below
Outputs:
- density: float32 [32, 64, 2048], P('rad', 'ell')
- displacement: float32 [32, 64, 2048], P('rad', 'ell')
The draws below stay inside these ranges and needn't reach their ends.
Inputs may be any that keep to these rules, and one draw needn't show every extreme that they name: mode_counts[0] is 256.
All inputs are finite; a program needn't handle non-finite values.
Results may differ from the reference program's by a relative error of at most 0.0029.
Values may be sent and summed in bfloat16 or wider, within the bound.
No kernel may reach another device: no remote copies, remote signals or barrier semaphores. Data moves between devices by JAX's collectives and lax.ppermute only.
A program may use at most 256 MiB of HBM per device.

```python
import math
import jax
import jax.numpy as jnp
from jax import lax

L = 1536
NR = 256
NSIDE = 512
NR_DEV = 32
PAIRS = 768
SLOTS = 1537
SH = 32
RH = 32
PIX = 2048


def draw_mode_counts(key, part):
    key = jax.random.fold_in(key, 7)
    degrees = jnp.arange(L, dtype=jnp.int32)
    trend_line = NR - degrees * 3 * NR // (4 * L)
    jitter = jax.random.randint(key, (L,), -(NR // 8), NR // 8 + 1, dtype=jnp.int32)
    counts = jnp.clip(trend_line + jitter, 1, NR)
    return jnp.where(degrees == 0, NR, counts).astype(jnp.int32)


def levels(key, dims, cuts, low, top_value):
    gain, own = 1.0, jax.random.fold_in(key, 6)
    for axis_at, shards_of in cuts:
        heights = jnp.exp(jax.random.uniform(jax.random.fold_in(own, axis_at), (shards_of,), jnp.float32, low / len(cuts), top_value / len(cuts)))
        gain = gain * jnp.repeat(heights, dims[axis_at] // shards_of).reshape([-1 if axis == axis_at else 1 for axis in range(len(dims))])
    return gain


def normal_values(stream_key, dims, deviation, reach, split=(), held_as=jnp.bfloat16):
    drawn = jax.random.normal(stream_key, dims, jnp.float32) * deviation
    if len(split) > 0:
        drawn = levels(stream_key, dims, split, -0.22, 0.18) * drawn
    return jnp.clip(drawn, min=-reach, max=reach).astype(held_as)


def setup_inputs(seed: int = 0) -> dict:
    key_list = jax.random.split(jax.random.key(seed), 5)
    return {
        "coefficients": normal_values(key_list[0], (2, NR, PAIRS, SLOTS), 0.025, 0.14941406, ((1, 8), (2, 32))),
        "legendre": normal_values(key_list[1], (RH, PAIRS, SLOTS), L ** -0.5, 0.15625, ((1, 32),)),
        "bessel": normal_values(key_list[2], (2, SH, NR, L), NR ** -0.5, 0.375, ((2, 8), (3, 32))),
        "mode_counts": draw_mode_counts(jax.random.fold_in(key_list[4], 71), 0),
    }


ell_block = 16


def sheared_block(table, start):
    half_count = table.shape[-2]
    pair_index = jnp.arange(half_count, dtype=jnp.int32)
    degrees = start + jnp.arange(ell_block, dtype=jnp.int32)
    offsets = degrees[None, :] - pair_index[:, None]
    lead_ones = (1,) * (table.ndim - 2)
    index_table = jnp.clip(offsets, 0, L).astype(jnp.int32).reshape(lead_ones + (half_count, ell_block))
    picked = jnp.take_along_axis(table, index_table, axis=table.ndim - 1)
    lower_part = jnp.where(offsets >= 0, picked, jnp.zeros_like(picked))
    upper_part = lax.dynamic_slice_in_dim(table, start + 1, ell_block, axis=table.ndim - 1)
    keep_upper = degrees[None, :] >= L - 1 - pair_index[:, None]
    upper_part = jnp.where(keep_upper, upper_part, jnp.zeros_like(upper_part))
    return jnp.concatenate([lower_part, upper_part], axis=table.ndim - 2)


def reference(coefficients, legendre, bessel, mode_counts):
    half_count = L // 2
    pair_index = jnp.arange(half_count, dtype=jnp.int32)
    orders = jnp.concatenate([pair_index, L - 1 - pair_index])
    groups = NR // NR_DEV
    north = legendre.shape[0]
    mode_index = jnp.arange(NR, dtype=jnp.int32)

    def step(totals, block_id):
        start = block_id * ell_block
        degrees = start + jnp.arange(ell_block, dtype=jnp.int32)
        kept = lax.dynamic_slice_in_dim(mode_counts, start, ell_block)
        live = mode_index[:, None] < kept[None, :]
        coeff_block = sheared_block(coefficients, start).astype(jnp.float32)
        coeff_block = jnp.where(live[None, :, None, :], coeff_block, jnp.zeros_like(coeff_block))
        radial_table = lax.dynamic_slice_in_dim(bessel, start, ell_block, axis=3).astype(jnp.float32)
        coeff_groups = coeff_block.reshape(2, groups, NR_DEV, L, ell_block)
        table_groups = radial_table.reshape(2, SH, groups, NR_DEV, ell_block)
        radial = jnp.einsum('cbnml,fsbnl->bmcfsl', coeff_groups, table_groups, precision=lax.Precision.HIGHEST)
        radial = lax.optimization_barrier(radial.astype(jnp.bfloat16)).astype(jnp.float32)
        summed = jnp.sum(radial, axis=0)
        angular = sheared_block(legendre, start).astype(jnp.float32)
        parity = (degrees[None, :] + orders[:, None]) % 2
        even_part = jnp.where(parity[None] == 0, angular, jnp.zeros_like(angular))
        both_parts = jnp.concatenate([even_part, angular - even_part], axis=0)
        update = jnp.einsum('mcfsl,rml->mrcfs', summed, both_parts, precision=lax.Precision.HIGHEST)
        return totals + update, None

    initial = jnp.zeros((L, 2 * north, 2, 2, SH), jnp.float32)
    totals, _ = lax.scan(step, initial, jnp.arange(L // ell_block, dtype=jnp.int32))
    by_order = jnp.concatenate([totals[:half_count], totals[half_count:][::-1]], axis=0)
    even_sum = by_order[:, :north]
    odd_sum = by_order[:, north:]
    fourier = jnp.concatenate([even_sum + odd_sum, (even_sum - odd_sum)[:, ::-1]], axis=1)

    all_orders = jnp.arange(L, dtype=jnp.int32)
    cycle_ids = jnp.arange(2 * north, dtype=jnp.int32)
    cycle_number = jnp.where(cycle_ids < north, 2 * NSIDE - north + cycle_ids, 2 * NSIDE + 1 + cycle_ids - north)
    shifts = (cycle_number - NSIDE + 1) % 2
    turn = (shifts[None, :] * all_orders[:, None]) % (8 * NSIDE)
    twist = (2.0 * math.pi / (8 * NSIDE)) * turn.astype(jnp.float32)
    twist_cos = jnp.cos(twist)[:, :, None, None]
    twist_sin = jnp.sin(twist)[:, :, None, None]
    weight = jnp.where(all_orders == 0, 1.0, 2.0).astype(jnp.float32)[:, None, None, None]
    real_part = fourier[:, :, 0]
    imag_part = fourier[:, :, 1]
    turned_real = weight * (real_part * twist_cos + imag_part * twist_sin)
    turned_imag = weight * (imag_part * twist_cos - real_part * twist_sin)
    pixel_ids = jnp.arange(PIX, dtype=jnp.int32)
    phase = (all_orders[:, None] * (pixel_ids[None, :] + 1)) % (4 * NSIDE)
    angle = (2.0 * math.pi / (4 * NSIDE)) * phase.astype(jnp.float32)
    field = jnp.einsum('mgfs,mj->fsgj', turned_real, jnp.cos(angle), precision=lax.Precision.HIGHEST)
    field = field - jnp.einsum('mgfs,mj->fsgj', turned_imag, jnp.sin(angle), precision=lax.Precision.HIGHEST)
    return field[0], field[1]
```

```python
import functools
import math

import jax
import jax.numpy as jnp
import numpy as np
from jax import lax
from jax.experimental import pallas as pl
from jax.experimental.pallas import tpu as pltpu
from jax.sharding import PartitionSpec as P

L = 1536
HALF_PIX = 1024
PAIR_DEV = 24
MODES_DEV = 32
STEPS = 14
GROUPS = 32
SPAN = STEPS * GROUPS
KPAD = 512
BF = jnp.bfloat16
F32 = jnp.float32


def step_info(k, e):
    p0 = PAIR_DEV * e
    n_low = 12 - p0 // 128
    first_high = (L - PAIR_DEV - p0) // 128
    is_low = k < n_low
    high_block = k - n_low + first_high
    return p0, n_low, is_low, high_block


def window_low(k, e):
    _, _, is_low, high_block = step_info(k, e)
    return jnp.where(is_low, jnp.maximum(k - 1, 0), jnp.minimum(high_block, 11))


def window_high(k, e):
    _, _, is_low, high_block = step_info(k, e)
    return jnp.where(is_low, k, jnp.minimum(high_block, 11) + 1)


def butterfly(parts, lane):
    parts = list(parts)
    for bit in range(5):
        distance = 4 << bit
        upper = (lane & distance) != 0
        for low in range(32):
            if low & (1 << bit):
                continue
            high = low | (1 << bit)
            first, second = parts[low], parts[high]
            parts[low] = jnp.where(upper, pltpu.roll(second, distance, 1), first)
            parts[high] = jnp.where(upper, second, pltpu.roll(first, 128 - distance, 1))
    return parts


def coeff_kernel(e_ref, first_ref, second_ref, out_ref, stage):
    k = pl.program_id(0)
    _, _, is_low, _ = step_info(k, e_ref[0])
    lane = lax.broadcasted_iota(jnp.int32, (8, 128), 1)
    row = lax.broadcasted_iota(jnp.int32, (8, 128), 0)

    def run(shifted):
        def part(c, carry):
            for tile in range(3):
                parts = []
                for n in range(MODES_DEV):
                    a = first_ref[c, n].astype(F32)[8 * tile : 8 * tile + 8]
                    b = second_ref[c, n].astype(F32)[8 * tile : 8 * tile + 8]
                    parts.append(shifted(a, b, tile))
                parts = butterfly(parts, lane)
                for g in range(GROUPS):
                    at = pl.multiple_of(c * PAIR_DEV + 8 * tile, 8)
                    stage[g, pl.ds(at, 8), :] = parts[g]
            return carry

        lax.fori_loop(0, 2, part, 0)

    @pl.when(is_low)
    def _():
        def shifted(a, b, tile):
            a = pltpu.roll(a, 8 * tile, 1, stride=1, stride_axis=0)
            b = pltpu.roll(b, 8 * tile, 1, stride=1, stride_axis=0)
            return jnp.where(lane >= row + 8 * tile, b, a)

        run(shifted)

    @pl.when(jnp.logical_not(is_low))
    def _():
        def shifted(a, b, tile):
            return jnp.where(lane < 127, pltpu.roll(a, 127, 1), pltpu.roll(b, 127, 1))

        run(shifted)

    for g in range(GROUPS):
        out_ref[0, g] = stage[g].astype(BF)


def coeff_blocks(e, coefficients):
    block = (2, MODES_DEV, PAIR_DEV, 128)
    return pl.pallas_call(
        coeff_kernel,
        out_shape=jax.ShapeDtypeStruct((STEPS, GROUPS, 2 * PAIR_DEV, 128), BF),
        grid_spec=pltpu.PrefetchScalarGridSpec(
            num_scalar_prefetch=1,
            grid=(STEPS,),
            in_specs=[
                pl.BlockSpec(block, lambda k, s: (0, 0, 0, window_low(k, s[0]))),
                pl.BlockSpec(block, lambda k, s: (0, 0, 0, window_high(k, s[0]))),
            ],
            out_specs=pl.BlockSpec((1, GROUPS, 2 * PAIR_DEV, 128), lambda k, s: (k, 0, 0, 0)),
            scratch_shapes=[pltpu.VMEM((GROUPS, 2 * PAIR_DEV, 128), F32)],
        ),
        compiler_params=pltpu.CompilerParams(vmem_limit_bytes=48 * 2**20),
        name="coeff_blocks",
    )(e, coefficients, coefficients)


def angular_kernel(e_ref, first_ref, second_ref, pick_ref, out_ref, stage, wide):
    k = pl.program_id(0)
    e = e_ref[0]
    p0, _, is_low, high_block = step_info(k, e)
    quarter = k % 4
    lane = lax.broadcasted_iota(jnp.int32, (PAIR_DEV, 128), 1)
    row = lax.broadcasted_iota(jnp.int32, (PAIR_DEV, 128), 0)

    def run(shifted, keep):
        for r in range(32):
            value = shifted(first_ref[r].astype(F32), second_ref[r].astype(F32))
            value = jnp.where(keep, value, 0.0)
            stage[pl.ds(r, PAIR_DEV, stride=32), :] = value

    @pl.when(jnp.logical_and(is_low, k < STEPS))
    def _():
        def shifted(a, b):
            a = pltpu.roll(a, 0, 1, stride=1, stride_axis=0)
            b = pltpu.roll(b, 0, 1, stride=1, stride_axis=0)
            return jnp.where(lane >= row, b, a)

        offset = 128 * k + lane
        run(shifted, (offset >= row) & (offset < L - p0))

    @pl.when(jnp.logical_and(jnp.logical_not(is_low), k < STEPS))
    def _():
        def shifted(a, b):
            return jnp.where(lane < 127, pltpu.roll(a, 127, 1), pltpu.roll(b, 127, 1))

        degree = 128 * high_block + lane
        run(shifted, (degree >= L - 1 - p0 - row) & (degree < L))

    @pl.when(k >= STEPS)
    def _():
        stage[...] = jnp.zeros_like(stage)

    for q in range(4):
        @pl.when(quarter == q)
        def _():
            wide[:, 128 * q : 128 * q + 128] = stage[...].astype(BF)

    @pl.when(quarter == 3)
    def _():
        for j in range(4):
            picked = jnp.dot(
                wide[...], pick_ref[:, 128 * j : 128 * j + 128], preferred_element_type=F32
            )
            for i in range(PAIR_DEV):
                out_ref[i, 32 * j : 32 * j + 32, :] = picked[32 * i : 32 * i + 32].astype(BF)


def angular_blocks(e, legendre):
    block = (32, PAIR_DEV, 128)
    pick = np.zeros((512, 512), np.float32)
    for q in range(4):
        for g in range(32):
            for j in range(4):
                pick[128 * q + 4 * g + j, 128 * j + 32 * q + g] = 1.0
    return pl.pallas_call(
        angular_kernel,
        out_shape=jax.ShapeDtypeStruct((PAIR_DEV, 128, KPAD), BF),
        grid_spec=pltpu.PrefetchScalarGridSpec(
            num_scalar_prefetch=1,
            grid=(16,),
            in_specs=[
                pl.BlockSpec(block, lambda k, s: (0, 0, window_low(jnp.minimum(k, STEPS - 1), s[0]))),
                pl.BlockSpec(block, lambda k, s: (0, 0, window_high(jnp.minimum(k, STEPS - 1), s[0]))),
                pl.BlockSpec((512, 512), lambda k, s: (0, 0)),
            ],
            out_specs=pl.BlockSpec((PAIR_DEV, 128, 128), lambda k, s: (0, 0, k // 4)),
            scratch_shapes=[pltpu.VMEM((PAIR_DEV * 32, 128), F32), pltpu.VMEM((PAIR_DEV * 32, 512), BF)],
        ),
        compiler_params=pltpu.CompilerParams(vmem_limit_bytes=48 * 2**20),
        name="angular_blocks",
    )(e, legendre, legendre, jnp.asarray(pick, BF))


def sums_kernel(e_ref, twist_ref, coeff_ref, table_ref, angular_ref, out_ref, left, right, turned):
    k = pl.program_id(0)
    e = e_ref[0]
    p0, n_low, is_low, high_block = step_info(k, e)
    base = jnp.where(is_low, p0 // 4 + GROUPS * k, GROUPS * jnp.minimum(high_block, 11))
    lane = lax.broadcasted_iota(jnp.int32, (64, 128), 1)
    slots = [(lane & 3) == j for j in range(4)]

    def group(g, carry):
        table = table_ref[jnp.minimum(base + g, L // 4 - 1)]
        weights = jnp.concatenate(
            [jnp.where(slots[j], table, jnp.zeros_like(table)) for j in range(4)], axis=0
        )
        radial = lax.dot_general(
            coeff_ref[0, g], weights, (((1,), (1,)), ((), ())), preferred_element_type=F32
        )
        radial = radial.astype(BF).astype(F32)
        at = k * GROUPS + g
        left[pl.ds(at, 48, stride=SPAN), :] = radial[:, :128]
        right[pl.ds(at, 48, stride=SPAN), :] = radial[:, 128:]
        return carry

    lax.fori_loop(0, GROUPS, group, 0, unroll=4)

    @pl.when(k == STEPS - 1)
    def _():
        slot = lax.broadcasted_iota(jnp.int32, (64, SPAN), 1)
        low_slot = slot < GROUPS * n_low
        near = lax.broadcasted_iota(jnp.int32, (32, 128), 1) < 64
        even_row = (lax.broadcasted_iota(jnp.int32, (32, 128), 0) & 1) == 0

        def order(i, carry):
            first = angular_ref[i, 0:64, 0:SPAN]
            second = angular_ref[i, 64:128, 0:SPAN]
            zero = jnp.zeros_like(first)
            first = jnp.concatenate(
                [jnp.where(low_slot, first, zero), jnp.where(low_slot, zero, first)], axis=0
            )
            second = jnp.concatenate(
                [jnp.where(low_slot, second, zero), jnp.where(low_slot, zero, second)], axis=0
            )
            folded = [[None, None], [None, None]]
            for c in range(2):
                at = pl.multiple_of((c * PAIR_DEV + i) * SPAN, 8)
                one = jnp.dot(first, left[pl.ds(at, SPAN), :].astype(BF), preferred_element_type=F32)
                two = jnp.dot(second, right[pl.ds(at, SPAN), :].astype(BF), preferred_element_type=F32)
                both = one + two
                for seg in range(2):
                    total = jnp.where(near, both[64 * seg : 64 * seg + 32], both[64 * seg + 32 : 64 * seg + 64])
                    other = pltpu.roll(total, 64, 1)
                    sign = jnp.where((i + seg) % 2 == 0, 1.0, -1.0)
                    folded[c][seg] = jnp.where(near, total + other, (other - total) * sign)
            for seg in range(2):
                scale = twist_ref[2, seg * PAIR_DEV + i]
                cos = jnp.where(even_row, twist_ref[0, seg * PAIR_DEV + i], scale)
                sin = jnp.where(even_row, twist_ref[1, seg * PAIR_DEV + i], 0.0)
                real, imag = folded[0][seg], folded[1][seg]
                turned[pl.ds(seg * 48 + i, 32, stride=96), :] = real * cos + imag * sin
                turned[pl.ds(seg * 48 + PAIR_DEV + i, 32, stride=96), :] = imag * cos - real * sin
            return carry

        lax.fori_loop(0, PAIR_DEV, order, 0)

        def pair(q, carry):
            rows = [
                jnp.transpose(turned[pl.ds(pl.multiple_of((2 * q + d) * 96, 8), 96), :])
                for d in range(2)
            ]
            for owner in range(8):
                north = [x[8 * owner : 8 * owner + 8] for x in rows]
                south = [x[64 + 8 * owner : 72 + 8 * owner] for x in rows]
                out_ref[owner, q] = jnp.concatenate(north, axis=0).astype(BF)
                out_ref[owner, 31 - q] = jnp.concatenate(south[::-1], axis=0).astype(BF)
            return carry

        lax.fori_loop(0, 16, pair, 0)


def cycle_sums(e, twist, coeffs, table, angular):
    return pl.pallas_call(
        sums_kernel,
        out_shape=jax.ShapeDtypeStruct((8, 32, 16, 96), BF),
        grid_spec=pltpu.PrefetchScalarGridSpec(
            num_scalar_prefetch=2,
            grid=(STEPS,),
            in_specs=[
                pl.BlockSpec((1, GROUPS, 48, 128), lambda k, s, t: (k, 0, 0, 0)),
                pl.BlockSpec((L // 4, 64, 128), lambda k, s, t: (0, 0, 0), pipeline_mode=pl.Buffered(1)),
                pl.BlockSpec((PAIR_DEV, 128, KPAD), lambda k, s, t: (0, 0, 0), pipeline_mode=pl.Buffered(1)),
            ],
            out_specs=pl.BlockSpec((8, 32, 16, 96), lambda k, s, t: (0, 0, 0, 0)),
            scratch_shapes=[
                pltpu.VMEM((48 * SPAN, 128), F32),
                pltpu.VMEM((48 * SPAN, 128), F32),
                pltpu.VMEM((32 * 96, 128), F32),
            ],
        ),
        compiler_params=pltpu.CompilerParams(vmem_limit_bytes=56 * 2**20),
        name="cycle_sums",
    )(e, twist, coeffs, table, angular)


SOURCES_STEP = 8


def pixels_kernel(in_ref, basis_ref, dens_ref, disp_ref, total):
    step = pl.program_id(0)
    col = lax.broadcasted_iota(jnp.int32, (16, 96), 1)
    order = col % PAIR_DEV
    odd = (order + jnp.where(col >= 48, 1, 0)) % 2 == 1
    acc = None
    for source in range(SOURCES_STEP):
        value = in_ref[0, source].astype(F32)
        for radial in range(1, 8):
            value = value + in_ref[radial, source].astype(F32)
        top = value.astype(BF).astype(F32)
        rest = value - top
        rows = jnp.concatenate(
            [
                jnp.where(odd, 0.0, top),
                jnp.where(odd, top, 0.0),
                jnp.where(odd, 0.0, rest),
                jnp.where(odd, rest, 0.0),
            ],
            axis=0,
        ).astype(BF)
        part = jnp.dot(rows, basis_ref[source], preferred_element_type=F32)
        part = part[0:32] + part[32:64]
        acc = part if acc is None else acc + part

    @pl.when(step == 0)
    def _():
        total[...] = acc

    @pl.when(step > 0)
    def _():
        total[...] += acc

    @pl.when(step == pl.num_programs(0) - 1)
    def _():
        even, odd_part = total[0:16], total[16:32]
        near, far = even + odd_part, even - odd_part
        for cycle in range(2):
            for shell in range(4):
                at = cycle * 8 + shell
                for ref, row in ((dens_ref, at), (disp_ref, at + 4)):
                    ref[shell, cycle : cycle + 1, 0:HALF_PIX] = near[row : row + 1]
                    ref[shell, cycle : cycle + 1, HALF_PIX:] = far[row : row + 1]


def pixel_basis():
    source = np.arange(32)[:, None, None]
    i = np.arange(PAIR_DEV)[None, None, :]
    low = PAIR_DEV * source + i
    orders = np.concatenate([low, L - 1 - low], axis=1)
    phase = (orders[..., None] * (np.arange(HALF_PIX) + 1)) % 2048
    angle = 2.0 * math.pi / 2048 * phase
    basis = np.stack([np.cos(angle), -np.sin(angle)], axis=2)
    return basis.reshape(32, 96, HALF_PIX).astype(jnp.bfloat16)


def pixels(received):
    out = jax.ShapeDtypeStruct((4, 2, 2 * HALF_PIX), F32)
    spec = pl.BlockSpec((4, 2, 2 * HALF_PIX), lambda k: (0, 0, 0))
    return pl.pallas_call(
        pixels_kernel,
        out_shape=(out, out),
        grid=(32 // SOURCES_STEP,),
        in_specs=[
            pl.BlockSpec((8, SOURCES_STEP, 16, 96), lambda k: (0, k, 0, 0)),
            pl.BlockSpec((SOURCES_STEP, 96, HALF_PIX), lambda k: (k, 0, 0)),
        ],
        out_specs=(spec, spec),
        scratch_shapes=[pltpu.VMEM((32, HALF_PIX), F32)],
        compiler_params=pltpu.CompilerParams(vmem_limit_bytes=48 * 2**20),
        name="pixels",
    )(received, jnp.asarray(pixel_basis()))


def radial_table(bessel, mode_counts):
    width = bessel.shape[3]
    counts = lax.dynamic_slice_in_dim(mode_counts, lax.axis_index("ell") * width, width)
    modes = lax.axis_index("rad") * MODES_DEV + jnp.arange(MODES_DEV, dtype=jnp.int32)
    live = modes[:, None] < counts[None, :]
    table = jnp.where(live, bessel, jnp.zeros_like(bessel))
    table = table.reshape(2, 8, 4, MODES_DEV, width // 4, 4)
    table = table.transpose(4, 1, 0, 2, 3, 5)
    return table.reshape(width // 4, 64, 4 * MODES_DEV)


def twist_table():
    low = np.arange(L // 2).reshape(32, PAIR_DEV)
    orders = np.concatenate([low, L - 1 - low], axis=1)
    weight = np.where(orders == 0, 1.0, 2.0)
    angle = 2.0 * math.pi / 4096 * orders
    return np.stack([weight * np.cos(angle), weight * np.sin(angle), weight], axis=1).astype(np.float32)


def local(coefficients, legendre, bessel, mode_counts):
    e = lax.axis_index("ell")
    e_arr = e.reshape(1).astype(jnp.int32)
    twist = lax.dynamic_index_in_dim(jnp.asarray(twist_table()), e, 0, keepdims=False)
    table = lax.all_gather(radial_table(bessel, mode_counts), "ell", axis=0, tiled=True)
    coeffs = coeff_blocks(e_arr, coefficients)
    angular = angular_blocks(e_arr, legendre)
    sums = cycle_sums(e_arr, twist, coeffs, table, angular)
    received = lax.all_to_all(
        sums.reshape(256, 16, 96), ("rad", "ell"), split_axis=0, concat_axis=0, tiled=True
    )
    return pixels(received.reshape(8, 32, 16, 96))


def solution(mesh):
    in_specs = (P(None, "rad", "ell", None), P(None, "ell", None), P(None, None, "rad", "ell"), P())
    out_specs = (P("rad", "ell", None), P("rad", "ell", None))
    return jax.shard_map(local, mesh=mesh, in_specs=in_specs, out_specs=out_specs, check_vma=False)
```

```python
import functools
import math

import jax
import jax.numpy as jnp
import numpy as np
from jax import lax
from jax.experimental import pallas as pl
from jax.experimental.pallas import tpu as pltpu
from jax.sharding import PartitionSpec as P

L = 1536
HALF_PIX = 1024
PAIR_DEV = 24
MODES_DEV = 32
STEPS = 14
GROUPS = 32
SPAN = STEPS * GROUPS
PITCH = SPAN + 8
KPAD = 512
BF = jnp.bfloat16
F32 = jnp.float32


def step_info(k, e):
    p0 = PAIR_DEV * e
    n_low = 12 - p0 // 128
    first_high = (L - PAIR_DEV - p0) // 128
    is_low = k < n_low
    high_block = k - n_low + first_high
    return p0, n_low, is_low, high_block


def window_low(k, e):
    _, _, is_low, high_block = step_info(k, e)
    return jnp.where(is_low, jnp.maximum(k - 1, 0), jnp.minimum(high_block, 11))


def window_high(k, e):
    _, _, is_low, high_block = step_info(k, e)
    return jnp.where(is_low, k, jnp.minimum(high_block, 11) + 1)


def butterfly(parts, lane):
    parts = list(parts)
    for bit in range(5):
        distance = 4 << bit
        upper = (lane & distance) != 0
        for low in range(32):
            if low & (1 << bit):
                continue
            high = low | (1 << bit)
            first, second = parts[low], parts[high]
            parts[low] = jnp.where(upper, pltpu.roll(second, distance, 1), first)
            parts[high] = jnp.where(upper, second, pltpu.roll(first, 128 - distance, 1))
    return parts


def coeff_kernel(e_ref, first_ref, second_ref, out_ref, stage):
    k = pl.program_id(0)
    _, _, is_low, _ = step_info(k, e_ref[0])
    lane = lax.broadcasted_iota(jnp.int32, (8, 128), 1)
    row = lax.broadcasted_iota(jnp.int32, (8, 128), 0)

    def run(shifted):
        def part(c, carry):
            for tile in range(3):
                parts = []
                for n in range(MODES_DEV):
                    a = first_ref[c, n].astype(F32)[8 * tile : 8 * tile + 8]
                    b = second_ref[c, n].astype(F32)[8 * tile : 8 * tile + 8]
                    parts.append(shifted(a, b, tile))
                parts = butterfly(parts, lane)
                for g in range(GROUPS):
                    at = pl.multiple_of(c * PAIR_DEV + 8 * tile, 8)
                    stage[g, pl.ds(at, 8), :] = parts[g]
            return carry

        lax.fori_loop(0, 2, part, 0)

    @pl.when(is_low)
    def _():
        def shifted(a, b, tile):
            a = pltpu.roll(a, 8 * tile, 1, stride=1, stride_axis=0)
            b = pltpu.roll(b, 8 * tile, 1, stride=1, stride_axis=0)
            return jnp.where(lane >= row + 8 * tile, b, a)

        run(shifted)

    @pl.when(jnp.logical_not(is_low))
    def _():
        def shifted(a, b, tile):
            return jnp.where(lane < 127, pltpu.roll(a, 127, 1), pltpu.roll(b, 127, 1))

        run(shifted)

    for g in range(GROUPS):
        out_ref[0, g] = stage[g].astype(BF)


def coeff_blocks(e, coefficients):
    block = (2, MODES_DEV, PAIR_DEV, 128)
    return pl.pallas_call(
        coeff_kernel,
        out_shape=jax.ShapeDtypeStruct((STEPS, GROUPS, 2 * PAIR_DEV, 128), BF),
        grid_spec=pltpu.PrefetchScalarGridSpec(
            num_scalar_prefetch=1,
            grid=(STEPS,),
            in_specs=[
                pl.BlockSpec(block, lambda k, s: (0, 0, 0, window_low(k, s[0]))),
                pl.BlockSpec(block, lambda k, s: (0, 0, 0, window_high(k, s[0]))),
            ],
            out_specs=pl.BlockSpec((1, GROUPS, 2 * PAIR_DEV, 128), lambda k, s: (k, 0, 0, 0)),
            scratch_shapes=[pltpu.VMEM((GROUPS, 2 * PAIR_DEV, 128), F32)],
        ),
        compiler_params=pltpu.CompilerParams(vmem_limit_bytes=48 * 2**20),
        name="coeff_blocks",
    )(e, coefficients, coefficients)


def angular_kernel(e_ref, first_ref, second_ref, pick_ref, out_ref, stage, wide):
    k = pl.program_id(0)
    e = e_ref[0]
    p0, _, is_low, high_block = step_info(k, e)
    quarter = k % 4
    lane = lax.broadcasted_iota(jnp.int32, (PAIR_DEV, 128), 1)
    row = lax.broadcasted_iota(jnp.int32, (PAIR_DEV, 128), 0)

    def run(shifted, keep):
        for r in range(32):
            value = shifted(first_ref[r].astype(F32), second_ref[r].astype(F32))
            value = jnp.where(keep, value, 0.0)
            stage[pl.ds(r, PAIR_DEV, stride=32), :] = value

    @pl.when(jnp.logical_and(is_low, k < STEPS))
    def _():
        def shifted(a, b):
            a = pltpu.roll(a, 0, 1, stride=1, stride_axis=0)
            b = pltpu.roll(b, 0, 1, stride=1, stride_axis=0)
            return jnp.where(lane >= row, b, a)

        offset = 128 * k + lane
        run(shifted, (offset >= row) & (offset < L - p0))

    @pl.when(jnp.logical_and(jnp.logical_not(is_low), k < STEPS))
    def _():
        def shifted(a, b):
            return jnp.where(lane < 127, pltpu.roll(a, 127, 1), pltpu.roll(b, 127, 1))

        degree = 128 * high_block + lane
        run(shifted, (degree >= L - 1 - p0 - row) & (degree < L))

    @pl.when(k >= STEPS)
    def _():
        stage[...] = jnp.zeros_like(stage)

    for q in range(4):
        @pl.when(quarter == q)
        def _():
            wide[:, 128 * q : 128 * q + 128] = stage[...].astype(BF)

    @pl.when(quarter == 3)
    def _():
        for j in range(4):
            picked = jnp.dot(
                wide[...], pick_ref[:, 128 * j : 128 * j + 128], preferred_element_type=F32
            )
            for i in range(PAIR_DEV):
                out_ref[i, 32 * j : 32 * j + 32, :] = picked[32 * i : 32 * i + 32].astype(BF)


def angular_blocks(e, legendre):
    block = (32, PAIR_DEV, 128)
    pick = np.zeros((512, 512), np.float32)
    for q in range(4):
        for g in range(32):
            for j in range(4):
                pick[128 * q + 4 * g + j, 128 * j + 32 * q + g] = 1.0
    return pl.pallas_call(
        angular_kernel,
        out_shape=jax.ShapeDtypeStruct((PAIR_DEV, 128, KPAD), BF),
        grid_spec=pltpu.PrefetchScalarGridSpec(
            num_scalar_prefetch=1,
            grid=(16,),
            in_specs=[
                pl.BlockSpec(block, lambda k, s: (0, 0, window_low(jnp.minimum(k, STEPS - 1), s[0]))),
                pl.BlockSpec(block, lambda k, s: (0, 0, window_high(jnp.minimum(k, STEPS - 1), s[0]))),
                pl.BlockSpec((512, 512), lambda k, s: (0, 0)),
            ],
            out_specs=pl.BlockSpec((PAIR_DEV, 128, 128), lambda k, s: (0, 0, k // 4)),
            scratch_shapes=[pltpu.VMEM((PAIR_DEV * 32, 128), F32), pltpu.VMEM((PAIR_DEV * 32, 512), BF)],
        ),
        compiler_params=pltpu.CompilerParams(vmem_limit_bytes=48 * 2**20),
        name="angular_blocks",
    )(e, legendre, legendre, jnp.asarray(pick, BF))


def table_first(k, e):
    p0, _, is_low, high_block = step_info(k, e)
    return jnp.where(is_low, p0 // 4 + GROUPS * k, GROUPS * jnp.minimum(high_block, 11))


def table_start(k, e):
    return jnp.minimum(table_first(k, e), L // 4 - GROUPS)


def sums_kernel(
    e_ref, twist_ref, coeff_ref, table_ref, angular_hbm, out_ref, left, right, turned, angular_ref, sem
):
    k = pl.program_id(0)
    e = e_ref[0]
    _, n_low, _, _ = step_info(k, e)
    base = table_first(k, e) - table_start(k, e)
    fetch = pltpu.make_async_copy(angular_hbm, angular_ref, sem)

    @pl.when(k == 0)
    def _():
        fetch.start()

    lane = lax.broadcasted_iota(jnp.int32, (64, 128), 1)
    slots = [(lane & 3) == j for j in range(4)]

    def group(g, carry):
        table = table_ref[jnp.minimum(base + g, GROUPS - 1)]
        weights = jnp.concatenate(
            [jnp.where(slots[j], table, jnp.zeros_like(table)) for j in range(4)], axis=0
        )
        radial = lax.dot_general(
            coeff_ref[0, g], weights, (((1,), (1,)), ((), ())), preferred_element_type=F32
        )
        radial = radial.astype(BF).astype(F32)
        at = k * GROUPS + g
        left[pl.ds(at, 48, stride=PITCH), :] = radial[:, :128]
        right[pl.ds(at, 48, stride=PITCH), :] = radial[:, 128:]
        return carry

    lax.fori_loop(0, GROUPS, group, 0, unroll=True)

    @pl.when(k == STEPS - 1)
    def _():
        fetch.wait()
        slot = lax.broadcasted_iota(jnp.int32, (64, SPAN), 1)
        low_slot = slot < GROUPS * n_low
        near = lax.broadcasted_iota(jnp.int32, (32, 128), 1) < 64
        even_row = (lax.broadcasted_iota(jnp.int32, (32, 128), 0) & 1) == 0

        def order(i, carry):
            first = angular_ref[i, 0:64, 0:SPAN]
            second = angular_ref[i, 64:128, 0:SPAN]
            zero = jnp.zeros_like(first)
            first = jnp.concatenate(
                [jnp.where(low_slot, first, zero), jnp.where(low_slot, zero, first)], axis=0
            )
            second = jnp.concatenate(
                [jnp.where(low_slot, second, zero), jnp.where(low_slot, zero, second)], axis=0
            )
            folded = [[None, None], [None, None]]
            for c in range(2):
                at = pl.multiple_of((c * PAIR_DEV + i) * PITCH, 8)
                one = jnp.dot(first, left[pl.ds(at, SPAN), :].astype(BF), preferred_element_type=F32)
                two = jnp.dot(second, right[pl.ds(at, SPAN), :].astype(BF), preferred_element_type=F32)
                both = one + two
                for seg in range(2):
                    total = jnp.where(near, both[64 * seg : 64 * seg + 32], both[64 * seg + 32 : 64 * seg + 64])
                    other = pltpu.roll(total, 64, 1)
                    sign = jnp.where((i + seg) % 2 == 0, 1.0, -1.0)
                    folded[c][seg] = jnp.where(near, total + other, (other - total) * sign)
            for seg in range(2):
                scale = twist_ref[2, seg * PAIR_DEV + i]
                cos = jnp.where(even_row, twist_ref[0, seg * PAIR_DEV + i], scale)
                sin = jnp.where(even_row, twist_ref[1, seg * PAIR_DEV + i], 0.0)
                real, imag = folded[0][seg], folded[1][seg]
                turned[pl.ds(seg * 48 + i, 32, stride=96), :] = real * cos + imag * sin
                turned[pl.ds(seg * 48 + PAIR_DEV + i, 32, stride=96), :] = imag * cos - real * sin
            return carry

        lax.fori_loop(0, PAIR_DEV, order, 0, unroll=8)

        def pair(q, carry):
            rows = [
                jnp.transpose(turned[pl.ds(pl.multiple_of((2 * q + d) * 96, 8), 96), :])
                for d in range(2)
            ]
            for owner in range(8):
                north = [x[8 * owner : 8 * owner + 8] for x in rows]
                south = [x[64 + 8 * owner : 72 + 8 * owner] for x in rows]
                out_ref[owner, q] = jnp.concatenate(north, axis=0).astype(BF)
                out_ref[owner, 31 - q] = jnp.concatenate(south[::-1], axis=0).astype(BF)
            return carry

        lax.fori_loop(0, 16, pair, 0, unroll=4)


def cycle_sums(e, twist, coeffs, table, angular):
    return pl.pallas_call(
        sums_kernel,
        out_shape=jax.ShapeDtypeStruct((8, 32, 16, 96), BF),
        grid_spec=pltpu.PrefetchScalarGridSpec(
            num_scalar_prefetch=2,
            grid=(STEPS,),
            in_specs=[
                pl.BlockSpec((1, GROUPS, 48, 128), lambda k, s, t: (k, 0, 0, 0)),
                pl.BlockSpec(
                    (pl.Element(GROUPS), pl.Element(64), pl.Element(128)),
                    lambda k, s, t: (table_start(k, s[0]), 0, 0),
                ),
                pl.BlockSpec(memory_space=pl.ANY),
            ],
            out_specs=pl.BlockSpec((8, 32, 16, 96), lambda k, s, t: (0, 0, 0, 0)),
            scratch_shapes=[
                pltpu.VMEM((48 * PITCH, 128), F32),
                pltpu.VMEM((48 * PITCH, 128), F32),
                pltpu.VMEM((32 * 96, 128), F32),
                pltpu.VMEM((PAIR_DEV, 128, KPAD), BF),
                pltpu.SemaphoreType.DMA,
            ],
        ),
        compiler_params=pltpu.CompilerParams(vmem_limit_bytes=56 * 2**20),
        name="cycle_sums",
    )(e, twist, coeffs, table, angular)


SOURCES_STEP = 8


def pixels_kernel(in_ref, basis_ref, dens_ref, disp_ref, total):
    step = pl.program_id(0)
    col = lax.broadcasted_iota(jnp.int32, (16, 96), 1)
    order = col % PAIR_DEV
    odd = (order + jnp.where(col >= 48, 1, 0)) % 2 == 1
    acc = None
    for source in range(SOURCES_STEP):
        value = in_ref[0, source].astype(F32)
        for radial in range(1, 8):
            value = value + in_ref[radial, source].astype(F32)
        top = value.astype(BF).astype(F32)
        rest = value - top
        rows = jnp.concatenate(
            [
                jnp.where(odd, 0.0, top),
                jnp.where(odd, top, 0.0),
                jnp.where(odd, 0.0, rest),
                jnp.where(odd, rest, 0.0),
            ],
            axis=0,
        ).astype(BF)
        part = jnp.dot(rows, basis_ref[source], preferred_element_type=F32)
        part = part[0:32] + part[32:64]
        acc = part if acc is None else acc + part

    @pl.when(step == 0)
    def _():
        total[...] = acc

    @pl.when(step > 0)
    def _():
        total[...] += acc

    @pl.when(step == pl.num_programs(0) - 1)
    def _():
        even, odd_part = total[0:16], total[16:32]
        near, far = even + odd_part, even - odd_part
        for cycle in range(2):
            for shell in range(4):
                at = cycle * 8 + shell
                for ref, row in ((dens_ref, at), (disp_ref, at + 4)):
                    ref[shell, cycle : cycle + 1, 0:HALF_PIX] = near[row : row + 1]
                    ref[shell, cycle : cycle + 1, HALF_PIX:] = far[row : row + 1]


def pixel_basis():
    source = np.arange(32)[:, None, None]
    i = np.arange(PAIR_DEV)[None, None, :]
    low = PAIR_DEV * source + i
    orders = np.concatenate([low, L - 1 - low], axis=1)
    phase = (orders[..., None] * (np.arange(HALF_PIX) + 1)) % 2048
    angle = 2.0 * math.pi / 2048 * phase
    basis = np.stack([np.cos(angle), -np.sin(angle)], axis=2)
    return basis.reshape(32, 96, HALF_PIX).astype(jnp.bfloat16)


def pixels(received):
    out = jax.ShapeDtypeStruct((4, 2, 2 * HALF_PIX), F32)
    spec = pl.BlockSpec((4, 2, 2 * HALF_PIX), lambda k: (0, 0, 0))
    return pl.pallas_call(
        pixels_kernel,
        out_shape=(out, out),
        grid=(32 // SOURCES_STEP,),
        in_specs=[
            pl.BlockSpec((8, SOURCES_STEP, 16, 96), lambda k: (0, k, 0, 0)),
            pl.BlockSpec((SOURCES_STEP, 96, HALF_PIX), lambda k: (k, 0, 0)),
        ],
        out_specs=(spec, spec),
        scratch_shapes=[pltpu.VMEM((32, HALF_PIX), F32)],
        compiler_params=pltpu.CompilerParams(vmem_limit_bytes=48 * 2**20),
        name="pixels",
    )(received, jnp.asarray(pixel_basis()))


def radial_table(bessel, mode_counts):
    width = bessel.shape[3]
    counts = lax.dynamic_slice_in_dim(mode_counts, lax.axis_index("ell") * width, width)
    modes = lax.axis_index("rad") * MODES_DEV + jnp.arange(MODES_DEV, dtype=jnp.int32)
    live = modes[:, None] < counts[None, :]
    table = jnp.where(live, bessel, jnp.zeros_like(bessel))
    table = table.reshape(2, 8, 4, MODES_DEV, width // 4, 4)
    table = table.transpose(4, 1, 0, 2, 3, 5)
    return table.reshape(width // 4, 64, 4 * MODES_DEV)


def twist_table():
    low = np.arange(L // 2).reshape(32, PAIR_DEV)
    orders = np.concatenate([low, L - 1 - low], axis=1)
    weight = np.where(orders == 0, 1.0, 2.0)
    angle = 2.0 * math.pi / 4096 * orders
    return np.stack([weight * np.cos(angle), weight * np.sin(angle), weight], axis=1).astype(np.float32)


def local(coefficients, legendre, bessel, mode_counts):
    e = lax.axis_index("ell")
    e_arr = e.reshape(1).astype(jnp.int32)
    twist = lax.dynamic_index_in_dim(jnp.asarray(twist_table()), e, 0, keepdims=False)
    table = lax.all_gather(radial_table(bessel, mode_counts), "ell", axis=0, tiled=True)
    coeffs = coeff_blocks(e_arr, coefficients)
    angular = angular_blocks(e_arr, legendre)
    sums = cycle_sums(e_arr, twist, coeffs, table, angular)
    received = lax.all_to_all(
        sums.reshape(256, 16, 96), ("rad", "ell"), split_axis=0, concat_axis=0, tiled=True
    )
    return pixels(received.reshape(8, 32, 16, 96))


def solution(mesh):
    in_specs = (P(None, "rad", "ell", None), P(None, "ell", None), P(None, None, "rad", "ell"), P())
    out_specs = (P("rad", "ell", None), P("rad", "ell", None))
    return jax.shard_map(local, mesh=mesh, in_specs=in_specs, out_specs=out_specs, check_vma=False)
```

```python
import functools
import math

import jax
import jax.numpy as jnp
import numpy as np
from jax import lax
from jax.experimental import pallas as pl
from jax.experimental.pallas import tpu as pltpu
from jax.sharding import PartitionSpec as P

L = 1536
HALF_PIX = 1024
PAIR_DEV = 24
MODES_DEV = 32
STEPS = 14
GROUPS = 32
SPAN = STEPS * GROUPS
PITCH = SPAN + 8
KPAD = 512
ROW_PITCH = 40
PIECE = 12
SHIFTS = (0, 1, -1, 2)
BF = jnp.bfloat16
F32 = jnp.float32


def step_info(k, e):
    p0 = PAIR_DEV * e
    n_low = 12 - p0 // 128
    first_high = (L - PAIR_DEV - p0) // 128
    is_low = k < n_low
    high_block = k - n_low + first_high
    return p0, n_low, is_low, high_block


def window_low(k, e):
    _, _, is_low, high_block = step_info(k, e)
    return jnp.where(is_low, jnp.maximum(k - 1, 0), jnp.minimum(high_block, 11))


def window_high(k, e):
    _, _, is_low, high_block = step_info(k, e)
    return jnp.where(is_low, k, jnp.minimum(high_block, 11) + 1)


def butterfly(parts, lane):
    parts = list(parts)
    for bit in range(5):
        distance = 4 << bit
        upper = (lane & distance) != 0
        for low in range(32):
            if low & (1 << bit):
                continue
            high = low | (1 << bit)
            first, second = parts[low], parts[high]
            parts[low] = jnp.where(upper, pltpu.roll(second, distance, 1), first)
            parts[high] = jnp.where(upper, second, pltpu.roll(first, 128 - distance, 1))
    return parts


def coeff_kernel(e_ref, first_ref, second_ref, out_ref):
    k = pl.program_id(0)
    _, _, is_low, _ = step_info(k, e_ref[0])
    lane8 = lax.broadcasted_iota(jnp.int32, (8, 128), 1)
    row8 = lax.broadcasted_iota(jnp.int32, (8, 128), 0)
    lane = lax.broadcasted_iota(jnp.int32, (16, 128), 1)

    def run(shifted):
        for tile in range(3):
            parts = []
            for n in range(MODES_DEV):
                halves = []
                for half in range(2):
                    c, sub = divmod(2 * tile + half, 3)
                    a = first_ref[c, n].astype(F32)[8 * sub : 8 * sub + 8]
                    b = second_ref[c, n].astype(F32)[8 * sub : 8 * sub + 8]
                    halves.append(shifted(a, b, sub))
                parts.append(jnp.concatenate(halves, axis=0).astype(BF))
            parts = butterfly(parts, lane)
            for g in range(GROUPS):
                out_ref[0, g, 16 * tile : 16 * tile + 16, :] = parts[g]

    @pl.when(is_low)
    def _():
        def shifted(a, b, sub):
            mixed = jnp.where(lane8 < 128 - 8 * sub - row8, b, a)
            return pltpu.roll(mixed, 8 * sub, 1, stride=1, stride_axis=0)

        run(shifted)

    @pl.when(jnp.logical_not(is_low))
    def _():
        def shifted(a, b, sub):
            return pltpu.roll(jnp.where(lane8 >= 1, a, b), 127, 1)

        run(shifted)


def coeff_blocks(e, coefficients):
    block = (2, MODES_DEV, PAIR_DEV, 128)
    return pl.pallas_call(
        coeff_kernel,
        out_shape=jax.ShapeDtypeStruct((STEPS, GROUPS, 2 * PAIR_DEV, 128), BF),
        grid_spec=pltpu.PrefetchScalarGridSpec(
            num_scalar_prefetch=1,
            grid=(STEPS,),
            in_specs=[
                pl.BlockSpec(block, lambda k, s: (0, 0, 0, window_low(k, s[0]))),
                pl.BlockSpec(block, lambda k, s: (0, 0, 0, window_high(k, s[0]))),
            ],
            out_specs=pl.BlockSpec((1, GROUPS, 2 * PAIR_DEV, 128), lambda k, s: (k, 0, 0, 0)),
        ),
        compiler_params=pltpu.CompilerParams(vmem_limit_bytes=48 * 2**20),
        name="coeff_blocks",
    )(e, coefficients, coefficients)


def angular_kernel(e_ref, first_ref, second_ref, pick_ref, out_ref, stage, wide):
    k = pl.program_id(0)
    e = e_ref[0]
    p0, _, is_low, high_block = step_info(k, e)
    quarter = k % 4
    lane = lax.broadcasted_iota(jnp.int32, (PAIR_DEV, 128), 1)
    row = lax.broadcasted_iota(jnp.int32, (PAIR_DEV, 128), 0)

    def run(shifted, keep):
        for r in range(32):
            value = shifted(first_ref[r].astype(F32), second_ref[r].astype(F32))
            value = jnp.where(keep, value, 0.0)
            stage[pl.ds(r, PAIR_DEV, stride=ROW_PITCH), :] = value

    @pl.when(jnp.logical_and(is_low, k < STEPS))
    def _():
        def shifted(a, b):
            mixed = jnp.where(lane < 128 - row, b, a)
            return pltpu.roll(mixed, 0, 1, stride=1, stride_axis=0)

        offset = 128 * k + lane
        run(shifted, (offset >= row) & (offset < L - p0))

    @pl.when(jnp.logical_and(jnp.logical_not(is_low), k < STEPS))
    def _():
        def shifted(a, b):
            return pltpu.roll(jnp.where(lane >= 1, a, b), 127, 1)

        degree = 128 * high_block + lane
        run(shifted, (degree >= L - 1 - p0 - row) & (degree < L))

    @pl.when(k >= STEPS)
    def _():
        stage[...] = jnp.zeros_like(stage)

    for q in range(4):
        @pl.when(quarter == q)
        def _():
            for i in range(PAIR_DEV):
                value = stage[ROW_PITCH * i : ROW_PITCH * i + 32, :].astype(BF)
                wide[32 * i : 32 * i + 32, 128 * q : 128 * q + 128] = value

    @pl.when(quarter == 3)
    def _():
        for j in range(4):
            picked = jnp.dot(
                wide[...], pick_ref[:, 128 * j : 128 * j + 128], preferred_element_type=F32
            )
            for i in range(PAIR_DEV):
                out_ref[i, 32 * j : 32 * j + 32, :] = picked[32 * i : 32 * i + 32].astype(BF)


def angular_blocks(e, legendre):
    block = (32, PAIR_DEV, 128)
    pick = np.zeros((512, 512), np.float32)
    for q in range(4):
        for g in range(32):
            for j in range(4):
                pick[128 * q + 4 * g + j, 128 * j + 32 * q + g] = 1.0
    return pl.pallas_call(
        angular_kernel,
        out_shape=jax.ShapeDtypeStruct((PAIR_DEV, 128, KPAD), BF),
        grid_spec=pltpu.PrefetchScalarGridSpec(
            num_scalar_prefetch=1,
            grid=(16,),
            in_specs=[
                pl.BlockSpec(block, lambda k, s: (0, 0, window_low(jnp.minimum(k, STEPS - 1), s[0]))),
                pl.BlockSpec(block, lambda k, s: (0, 0, window_high(jnp.minimum(k, STEPS - 1), s[0]))),
                pl.BlockSpec((512, 512), lambda k, s: (0, 0)),
            ],
            out_specs=pl.BlockSpec((PAIR_DEV, 128, 128), lambda k, s: (0, 0, k // 4)),
            scratch_shapes=[pltpu.VMEM((PAIR_DEV * ROW_PITCH, 128), F32), pltpu.VMEM((PAIR_DEV * 32, 512), BF)],
        ),
        compiler_params=pltpu.CompilerParams(vmem_limit_bytes=48 * 2**20),
        name="angular_blocks",
    )(e, legendre, legendre, jnp.asarray(pick, BF))


def table_first(k, e):
    p0, _, is_low, high_block = step_info(k, e)
    return jnp.where(is_low, p0 // 4 + GROUPS * k, GROUPS * jnp.minimum(high_block, 11))


def piece_owner(e, other_core, second, first):
    core = (e + other_core) % 2
    x, y = (e // 2) % 4, e // 8
    along_x = jnp.where(core == 0, SHIFTS[first], SHIFTS[second])
    along_y = jnp.where(core == 0, SHIFTS[second], SHIFTS[first])
    return (((y + 4 - along_y) % 4) * 4 + (x + 4 - along_x) % 4) * 2 + core


def sums_kernel(e_ref, twist_ref, coeff_ref, *refs):
    gathered, (angular_hbm, out_ref, left, right, turned, table_ref, angular_ref, sems, sem) = refs[:8], refs[8:]
    k = pl.program_id(0)
    e = e_ref[0]
    p0, n_low, _, _ = step_info(k, e)
    base = table_first(k, e)
    fetch = pltpu.make_async_copy(angular_hbm, angular_ref, sem)
    first_piece = p0 // 4 // PIECE

    @pl.when(k == 0)
    def _():
        for buffer in range(8):
            other_core, second = divmod(buffer, 4)
            for first in range(4):
                owner = piece_owner(e, other_core, second, first)

                @pl.when(owner >= first_piece)
                def _():
                    pltpu.make_async_copy(
                        gathered[buffer].at[pl.ds(first * PIECE, PIECE)],
                        table_ref.at[pl.ds(owner * PIECE, PIECE)],
                        sems.at[owner],
                    ).start()

        fetch.start()

    last_group = L // 4 - 1
    wait_from = jnp.where(
        k == 0, first_piece, jnp.minimum(p0 // 4 + GROUPS * k - 1, last_group) // PIECE + 1
    )
    wait_to = jnp.minimum(p0 // 4 + GROUPS * k + GROUPS - 1, last_group) // PIECE + 1

    def arrive(piece, carry):
        pltpu.make_async_copy(
            gathered[0].at[pl.ds(0, PIECE)], table_ref.at[pl.ds(piece * PIECE, PIECE)], sems.at[piece]
        ).wait()
        return carry

    lax.fori_loop(wait_from, wait_to, arrive, 0)

    lane = lax.broadcasted_iota(jnp.int32, (64, 128), 1)
    slots = [(lane & 3) == j for j in range(4)]

    def group(g, carry):
        table = table_ref[jnp.minimum(base + g, last_group)]
        weights = jnp.concatenate(
            [jnp.where(slots[j], table, jnp.zeros_like(table)) for j in range(4)], axis=0
        )
        radial = lax.dot_general(
            coeff_ref[0, g], weights, (((1,), (1,)), ((), ())), preferred_element_type=F32
        )
        radial = radial.astype(BF).astype(F32)
        at = k * GROUPS + g
        left[pl.ds(at, 48, stride=PITCH), :] = radial[:, :128]
        right[pl.ds(at, 48, stride=PITCH), :] = radial[:, 128:]
        return carry

    lax.fori_loop(0, GROUPS, group, 0, unroll=True)

    @pl.when(k == STEPS - 1)
    def _():
        fetch.wait()
        slot = lax.broadcasted_iota(jnp.int32, (64, SPAN), 1)
        low_slot = slot < GROUPS * n_low
        near = lax.broadcasted_iota(jnp.int32, (32, 128), 1) < 64
        even_row = (lax.broadcasted_iota(jnp.int32, (32, 128), 0) & 1) == 0

        def order(i, carry):
            first = angular_ref[i, 0:64, 0:SPAN]
            second = angular_ref[i, 64:128, 0:SPAN]
            zero = jnp.zeros_like(first)
            first = jnp.concatenate(
                [jnp.where(low_slot, first, zero), jnp.where(low_slot, zero, first)], axis=0
            )
            second = jnp.concatenate(
                [jnp.where(low_slot, second, zero), jnp.where(low_slot, zero, second)], axis=0
            )
            folded = [[None, None], [None, None]]
            for c in range(2):
                at = pl.multiple_of((c * PAIR_DEV + i) * PITCH, 8)
                one = jnp.dot(first, left[pl.ds(at, SPAN), :].astype(BF), preferred_element_type=F32)
                two = jnp.dot(second, right[pl.ds(at, SPAN), :].astype(BF), preferred_element_type=F32)
                both = one + two
                for seg in range(2):
                    total = jnp.where(near, both[64 * seg : 64 * seg + 32], both[64 * seg + 32 : 64 * seg + 64])
                    other = pltpu.roll(total, 64, 1)
                    sign = jnp.where((i + seg) % 2 == 0, 1.0, -1.0)
                    folded[c][seg] = jnp.where(near, total + other, (other - total) * sign)
            for seg in range(2):
                scale = twist_ref[2, seg * PAIR_DEV + i]
                cos = jnp.where(even_row, twist_ref[0, seg * PAIR_DEV + i], scale)
                sin = jnp.where(even_row, twist_ref[1, seg * PAIR_DEV + i], 0.0)
                real, imag = folded[0][seg], folded[1][seg]
                turned[pl.ds(seg * 48 + i, 32, stride=96), :] = real * cos + imag * sin
                turned[pl.ds(seg * 48 + PAIR_DEV + i, 32, stride=96), :] = imag * cos - real * sin
            return carry

        lax.fori_loop(0, PAIR_DEV, order, 0, unroll=8)

        def pair(q, carry):
            rows = [
                jnp.transpose(turned[pl.ds(pl.multiple_of((2 * q + d) * 96, 8), 96), :])
                for d in range(2)
            ]
            for owner in range(8):
                north = [x[8 * owner : 8 * owner + 8] for x in rows]
                south = [x[64 + 8 * owner : 72 + 8 * owner] for x in rows]
                out_ref[owner, q] = jnp.concatenate(north, axis=0).astype(BF)
                out_ref[owner, 31 - q] = jnp.concatenate(south[::-1], axis=0).astype(BF)
            return carry

        lax.fori_loop(0, 16, pair, 0, unroll=4)


def cycle_sums(e, twist, coeffs, gathered, angular):
    return pl.pallas_call(
        sums_kernel,
        out_shape=jax.ShapeDtypeStruct((8, 32, 16, 96), BF),
        grid_spec=pltpu.PrefetchScalarGridSpec(
            num_scalar_prefetch=2,
            grid=(STEPS,),
            in_specs=[
                pl.BlockSpec((1, GROUPS, 48, 128), lambda k, s, t: (k, 0, 0, 0)),
                *[pl.BlockSpec(memory_space=pl.ANY)] * 9,
            ],
            out_specs=pl.BlockSpec((8, 32, 16, 96), lambda k, s, t: (0, 0, 0, 0)),
            scratch_shapes=[
                pltpu.VMEM((48 * PITCH, 128), F32),
                pltpu.VMEM((48 * PITCH, 128), F32),
                pltpu.VMEM((32 * 96, 128), F32),
                pltpu.VMEM((L // 4, 64, 128), BF),
                pltpu.VMEM((PAIR_DEV, 128, KPAD), BF),
                pltpu.SemaphoreType.DMA((32,)),
                pltpu.SemaphoreType.DMA,
            ],
        ),
        compiler_params=pltpu.CompilerParams(vmem_limit_bytes=56 * 2**20),
        name="cycle_sums",
    )(e, twist, coeffs, *gathered, angular)


SOURCES_STEP = 8


def pixels_kernel(in_ref, basis_ref, dens_ref, disp_ref, total):
    step = pl.program_id(0)
    col = lax.broadcasted_iota(jnp.int32, (16, 96), 1)
    order = col % PAIR_DEV
    odd = (order + jnp.where(col >= 48, 1, 0)) % 2 == 1
    acc = None
    for source in range(SOURCES_STEP):
        value = in_ref[0, source].astype(F32)
        for radial in range(1, 8):
            value = value + in_ref[radial, source].astype(F32)
        top = value.astype(BF).astype(F32)
        rest = value - top
        rows = jnp.concatenate(
            [
                jnp.where(odd, 0.0, top),
                jnp.where(odd, top, 0.0),
                jnp.where(odd, 0.0, rest),
                jnp.where(odd, rest, 0.0),
            ],
            axis=0,
        ).astype(BF)
        part = jnp.dot(rows, basis_ref[source], preferred_element_type=F32)
        part = part[0:32] + part[32:64]
        acc = part if acc is None else acc + part

    @pl.when(step == 0)
    def _():
        total[...] = acc

    @pl.when(step > 0)
    def _():
        total[...] += acc

    @pl.when(step == pl.num_programs(0) - 1)
    def _():
        even, odd_part = total[0:16], total[16:32]
        near, far = even + odd_part, even - odd_part
        for cycle in range(2):
            for shell in range(4):
                at = cycle * 8 + shell
                for ref, row in ((dens_ref, at), (disp_ref, at + 4)):
                    ref[shell, cycle : cycle + 1, 0:HALF_PIX] = near[row : row + 1]
                    ref[shell, cycle : cycle + 1, HALF_PIX:] = far[row : row + 1]


def pixel_basis():
    source = np.arange(32)[:, None, None]
    i = np.arange(PAIR_DEV)[None, None, :]
    low = PAIR_DEV * source + i
    orders = np.concatenate([low, L - 1 - low], axis=1)
    phase = (orders[..., None] * (np.arange(HALF_PIX) + 1)) % 2048
    angle = 2.0 * math.pi / 2048 * phase
    basis = np.stack([np.cos(angle), -np.sin(angle)], axis=2)
    return basis.reshape(32, 96, HALF_PIX).astype(jnp.bfloat16)


def pixels(received):
    out = jax.ShapeDtypeStruct((4, 2, 2 * HALF_PIX), F32)
    spec = pl.BlockSpec((4, 2, 2 * HALF_PIX), lambda k: (0, 0, 0))
    return pl.pallas_call(
        pixels_kernel,
        out_shape=(out, out),
        grid=(32 // SOURCES_STEP,),
        in_specs=[
            pl.BlockSpec((8, SOURCES_STEP, 16, 96), lambda k: (0, k, 0, 0)),
            pl.BlockSpec((SOURCES_STEP, 96, HALF_PIX), lambda k: (k, 0, 0)),
        ],
        out_specs=(spec, spec),
        scratch_shapes=[pltpu.VMEM((32, HALF_PIX), F32)],
        compiler_params=pltpu.CompilerParams(vmem_limit_bytes=48 * 2**20),
        name="pixels",
    )(received, jnp.asarray(pixel_basis()))


def table_kernel(r_ref, bessel_ref, counts_ref, out_ref, stage, grouped):
    width = bessel_ref.shape[3]
    mode = lax.broadcasted_iota(jnp.int32, (MODES_DEV, width), 0) + MODES_DEV * r_ref[0]
    live = mode < counts_ref[...]
    lane = lax.broadcasted_iota(jnp.int32, (8, 128), 1)
    for owner in range(8):
        for f in range(2):
            for shell in range(4):
                row = (owner * 8 + f * 4 + shell) * ROW_PITCH
                value = bessel_ref[f, owner * 4 + shell].astype(F32)
                stage[row : row + MODES_DEV, 0:width] = jnp.where(live, value, 0.0)

    def one(owner, carry):
        parts = [
            stage[pl.ds(owner * 8 * ROW_PITCH + n, 8, stride=ROW_PITCH), :] for n in range(MODES_DEV)
        ]
        parts = butterfly(parts, lane)
        for g in range(width // 4):
            grouped[g, pl.ds(pl.multiple_of(owner * 8, 8), 8), :] = parts[g]
        return carry

    lax.fori_loop(0, 8, one, 0, unroll=2)
    for g in range(width // 4):
        out_ref[g] = grouped[g].astype(BF)


def radial_table(bessel, mode_counts):
    width = bessel.shape[3]
    counts = lax.dynamic_slice_in_dim(mode_counts, lax.axis_index("ell") * width, width)
    return pl.pallas_call(
        table_kernel,
        out_shape=jax.ShapeDtypeStruct((width // 4, 64, 128), BF),
        grid_spec=pltpu.PrefetchScalarGridSpec(
            num_scalar_prefetch=1,
            grid=(1,),
            in_specs=[
                pl.BlockSpec(bessel.shape, lambda k, s: (0, 0, 0, 0)),
                pl.BlockSpec((1, width), lambda k, s: (0, 0)),
            ],
            out_specs=pl.BlockSpec((width // 4, 64, 128), lambda k, s: (0, 0, 0)),
            scratch_shapes=[
                pltpu.VMEM((64 * ROW_PITCH, 128), F32),
                pltpu.VMEM((width // 4, 64, 128), F32),
            ],
        ),
        compiler_params=pltpu.CompilerParams(vmem_limit_bytes=32 * 2**20),
        name="radial_table",
    )(lax.axis_index("rad").reshape(1).astype(jnp.int32), bessel, counts.reshape(1, width))


def ring_shift(value, shift, first):
    pairs = []
    for e in range(32):
        core, x, y = e % 2, (e // 2) % 4, e // 8
        if (core == 0) == first:
            x = (x + shift) % 4
        else:
            y = (y + shift) % 4
        pairs.append((e, (y * 4 + x) * 2 + core))
    return lax.ppermute(value, "ell", pairs)


def other_core(value):
    return lax.ppermute(value, "ell", [(e, e ^ 1) for e in range(32)])


def twist_table():
    low = np.arange(L // 2).reshape(32, PAIR_DEV)
    orders = np.concatenate([low, L - 1 - low], axis=1)
    weight = np.where(orders == 0, 1.0, 2.0)
    angle = 2.0 * math.pi / 4096 * orders
    return np.stack([weight * np.cos(angle), weight * np.sin(angle), weight], axis=1).astype(np.float32)


def local(coefficients, legendre, bessel, mode_counts):
    e = lax.axis_index("ell")
    e_arr = e.reshape(1).astype(jnp.int32)
    twist = lax.dynamic_index_in_dim(jnp.asarray(twist_table()), e, 0, keepdims=False)
    table = radial_table(bessel, mode_counts)
    moved = [ring_shift(table, shift, True) for shift in SHIFTS[1:]]
    angular = angular_blocks(e_arr, legendre)
    angular, *moved = lax.optimization_barrier((angular, *moved))
    own = jnp.concatenate([table, *moved], axis=0)
    far = [ring_shift(own, shift, False) for shift in SHIFTS[1:]]
    e_late, own = lax.optimization_barrier((e_arr, own))
    coeffs = coeff_blocks(e_late, coefficients)
    coeffs, *far = lax.optimization_barrier((coeffs, *far))
    mine = [own, *far]
    gathered = mine + [other_core(value) for value in mine]
    sums = cycle_sums(e_arr, twist, coeffs, gathered, angular)
    received = lax.all_to_all(
        sums.reshape(256, 16, 96), ("rad", "ell"), split_axis=0, concat_axis=0, tiled=True
    )
    return pixels(received.reshape(8, 32, 16, 96))


def solution(mesh):
    in_specs = (P(None, "rad", "ell", None), P(None, "ell", None), P(None, None, "rad", "ell"), P())
    out_specs = (P("rad", "ell", None), P("rad", "ell", None))
    return jax.shard_map(local, mesh=mesh, in_specs=in_specs, out_specs=out_specs, check_vma=False)
```

```python
import functools
import math

import jax
import jax.numpy as jnp
import numpy as np
from jax import lax
from jax.experimental import pallas as pl
from jax.experimental.pallas import tpu as pltpu
from jax.sharding import PartitionSpec as P

L = 1536
HALF_PIX = 1024
PAIR_DEV = 24
MODES_DEV = 32
STEPS = 14
GROUPS = 32
SPAN = STEPS * GROUPS
PITCH = SPAN + 8
KPAD = 512
ROW_PITCH = 40
PIECE = 12
SHIFTS = (0, 1, -1, 2)
BF = jnp.bfloat16
F32 = jnp.float32


def step_info(k, e):
    p0 = PAIR_DEV * e
    n_low = 12 - p0 // 128
    first_high = (L - PAIR_DEV - p0) // 128
    is_low = k < n_low
    high_block = k - n_low + first_high
    return p0, n_low, is_low, high_block


def window_low(k, e):
    _, _, is_low, high_block = step_info(k, e)
    return jnp.where(is_low, jnp.maximum(k - 1, 0), jnp.minimum(high_block, 11))


def window_high(k, e):
    _, _, is_low, high_block = step_info(k, e)
    return jnp.where(is_low, k, jnp.minimum(high_block, 11) + 1)


def butterfly(parts, lane):
    parts = list(parts)
    for bit in range(5):
        distance = 4 << bit
        upper = (lane & distance) != 0
        for low in range(32):
            if low & (1 << bit):
                continue
            high = low | (1 << bit)
            first, second = parts[low], parts[high]
            if distance == 64:
                swapped = pltpu.roll(jnp.where(upper, first, second), 64, 1)
                parts[low] = jnp.where(upper, swapped, first)
                parts[high] = jnp.where(upper, second, swapped)
                continue
            parts[low] = jnp.where(upper, pltpu.roll(second, distance, 1), first)
            parts[high] = jnp.where(upper, second, pltpu.roll(first, 128 - distance, 1))
    return parts


def coeff_kernel(e_ref, first_ref, second_ref, out_ref):
    k = pl.program_id(0)
    _, _, is_low, _ = step_info(k, e_ref[0])
    lane8 = lax.broadcasted_iota(jnp.int32, (8, 128), 1)
    row8 = lax.broadcasted_iota(jnp.int32, (8, 128), 0)
    lane = lax.broadcasted_iota(jnp.int32, (16, 128), 1)

    def run(shifted):
        for tile in range(3):
            parts = []
            for n in range(MODES_DEV):
                halves = []
                for half in range(2):
                    c, sub = divmod(2 * tile + half, 3)
                    a = first_ref[c, n].astype(F32)[8 * sub : 8 * sub + 8]
                    b = second_ref[c, n].astype(F32)[8 * sub : 8 * sub + 8]
                    halves.append(shifted(a, b, sub))
                parts.append(jnp.concatenate(halves, axis=0).astype(BF))
            parts = butterfly(parts, lane)
            for g in range(GROUPS):
                out_ref[0, g, 16 * tile : 16 * tile + 16, :] = parts[g]

    @pl.when(is_low)
    def _():
        def shifted(a, b, sub):
            mixed = jnp.where(lane8 < 128 - 8 * sub - row8, b, a)
            return pltpu.roll(mixed, 8 * sub, 1, stride=1, stride_axis=0)

        run(shifted)

    @pl.when(jnp.logical_not(is_low))
    def _():
        def shifted(a, b, sub):
            return pltpu.roll(jnp.where(lane8 >= 1, a, b), 127, 1)

        run(shifted)


def coeff_blocks(e, coefficients):
    block = (2, MODES_DEV, PAIR_DEV, 128)
    return pl.pallas_call(
        coeff_kernel,
        out_shape=jax.ShapeDtypeStruct((STEPS, GROUPS, 2 * PAIR_DEV, 128), BF),
        grid_spec=pltpu.PrefetchScalarGridSpec(
            num_scalar_prefetch=1,
            grid=(STEPS,),
            in_specs=[
                pl.BlockSpec(block, lambda k, s: (0, 0, 0, window_low(k, s[0]))),
                pl.BlockSpec(block, lambda k, s: (0, 0, 0, window_high(k, s[0]))),
            ],
            out_specs=pl.BlockSpec((1, GROUPS, 2 * PAIR_DEV, 128), lambda k, s: (k, 0, 0, 0)),
        ),
        compiler_params=pltpu.CompilerParams(vmem_limit_bytes=48 * 2**20),
        name="coeff_blocks",
    )(e, coefficients, coefficients)


def angular_kernel(e_ref, first_ref, second_ref, out_ref, stage, wide, pick_ref):
    k = pl.program_id(0)
    e = e_ref[0]
    p0, _, is_low, high_block = step_info(k, e)
    quarter = k % 4

    @pl.when(k == 0)
    def _():
        slot = lax.broadcasted_iota(jnp.int32, (512, 128), 0)
        column = lax.broadcasted_iota(jnp.int32, (512, 128), 1)
        group = 32 * (slot >> 7) + ((slot & 127) >> 2)
        for j in range(4):
            hit = (column == group) & ((slot & 3) == j)
            pick_ref[:, 128 * j : 128 * j + 128] = jnp.where(hit, 1.0, 0.0).astype(BF)

    lane = lax.broadcasted_iota(jnp.int32, (PAIR_DEV, 128), 1)
    row = lax.broadcasted_iota(jnp.int32, (PAIR_DEV, 128), 0)

    def run(shifted, keep):
        for r in range(32):
            value = shifted(first_ref[r].astype(F32), second_ref[r].astype(F32))
            value = jnp.where(keep, value, 0.0)
            stage[pl.ds(r, PAIR_DEV, stride=ROW_PITCH), :] = value

    @pl.when(jnp.logical_and(is_low, k < STEPS))
    def _():
        def shifted(a, b):
            mixed = jnp.where(lane < 128 - row, b, a)
            return pltpu.roll(mixed, 0, 1, stride=1, stride_axis=0)

        offset = 128 * k + lane
        run(shifted, (offset >= row) & (offset < L - p0))

    @pl.when(jnp.logical_and(jnp.logical_not(is_low), k < STEPS))
    def _():
        def shifted(a, b):
            return pltpu.roll(jnp.where(lane >= 1, a, b), 127, 1)

        degree = 128 * high_block + lane
        run(shifted, (degree >= L - 1 - p0 - row) & (degree < L))

    @pl.when(k >= STEPS)
    def _():
        stage[...] = jnp.zeros_like(stage)

    for q in range(4):
        @pl.when(quarter == q)
        def _():
            for i in range(PAIR_DEV):
                value = stage[ROW_PITCH * i : ROW_PITCH * i + 32, :].astype(BF)
                wide[32 * i : 32 * i + 32, 128 * q : 128 * q + 128] = value

    @pl.when(quarter == 3)
    def _():
        for j in range(4):
            picked = jnp.dot(
                wide[...], pick_ref[:, 128 * j : 128 * j + 128], preferred_element_type=F32
            )
            for i in range(PAIR_DEV):
                out_ref[i, 32 * j : 32 * j + 32, :] = picked[32 * i : 32 * i + 32].astype(BF)


def angular_blocks(e, legendre):
    block = (32, PAIR_DEV, 128)
    return pl.pallas_call(
        angular_kernel,
        out_shape=jax.ShapeDtypeStruct((PAIR_DEV, 128, KPAD), BF),
        grid_spec=pltpu.PrefetchScalarGridSpec(
            num_scalar_prefetch=1,
            grid=(16,),
            in_specs=[
                pl.BlockSpec(block, lambda k, s: (0, 0, window_low(jnp.minimum(k, STEPS - 1), s[0]))),
                pl.BlockSpec(block, lambda k, s: (0, 0, window_high(jnp.minimum(k, STEPS - 1), s[0]))),
            ],
            out_specs=pl.BlockSpec((PAIR_DEV, 128, 128), lambda k, s: (0, 0, k // 4)),
            scratch_shapes=[pltpu.VMEM((PAIR_DEV * ROW_PITCH, 128), F32), pltpu.VMEM((PAIR_DEV * 32, 512), BF), pltpu.VMEM((512, 512), BF)],
        ),
        compiler_params=pltpu.CompilerParams(vmem_limit_bytes=48 * 2**20),
        name="angular_blocks",
    )(e, legendre, legendre)


def table_first(k, e):
    p0, _, is_low, high_block = step_info(k, e)
    return jnp.where(is_low, p0 // 4 + GROUPS * k, GROUPS * jnp.minimum(high_block, 11))


def piece_owner(e, other_core, second, first):
    core = (e + other_core) % 2
    x, y = (e // 2) % 4, e // 8
    along_x = jnp.where(core == 0, SHIFTS[first], SHIFTS[second])
    along_y = jnp.where(core == 0, SHIFTS[second], SHIFTS[first])
    return (((y + 4 - along_y) % 4) * 4 + (x + 4 - along_x) % 4) * 2 + core


def sums_kernel(e_ref, twist_ref, coeff_ref, *refs):
    gathered, (angular_hbm, out_ref, left, right, turned, table_ref, angular_ref, sems, sem) = refs[:8], refs[8:]
    k = pl.program_id(0)
    e = e_ref[0]
    p0, n_low, _, _ = step_info(k, e)
    base = table_first(k, e)
    fetch = pltpu.make_async_copy(angular_hbm, angular_ref, sem)
    first_piece = p0 // 4 // PIECE

    @pl.when(k == 0)
    def _():
        for buffer in range(8):
            other_core, second = divmod(buffer, 4)
            for first in range(4):
                owner = piece_owner(e, other_core, second, first)

                @pl.when(owner >= first_piece)
                def _():
                    pltpu.make_async_copy(
                        gathered[buffer].at[pl.ds(first * PIECE, PIECE)],
                        table_ref.at[pl.ds(owner * PIECE, PIECE)],
                        sems.at[owner],
                    ).start()

        fetch.start()

    last_group = L // 4 - 1
    wait_from = jnp.where(
        k == 0, first_piece, jnp.minimum(p0 // 4 + GROUPS * k - 1, last_group) // PIECE + 1
    )
    wait_to = jnp.minimum(p0 // 4 + GROUPS * k + GROUPS - 1, last_group) // PIECE + 1

    def arrive(piece, carry):
        pltpu.make_async_copy(
            gathered[0].at[pl.ds(0, PIECE)], table_ref.at[pl.ds(piece * PIECE, PIECE)], sems.at[piece]
        ).wait()
        return carry

    lax.fori_loop(wait_from, wait_to, arrive, 0)

    lane = lax.broadcasted_iota(jnp.int32, (64, 128), 1)
    slots = [(lane & 3) == j for j in range(4)]

    def group(g, carry):
        table = table_ref[jnp.minimum(base + g, last_group)]
        weights = jnp.concatenate(
            [jnp.where(slots[j], table, jnp.zeros_like(table)) for j in range(4)], axis=0
        )
        radial = lax.dot_general(
            coeff_ref[0, g], weights, (((1,), (1,)), ((), ())), preferred_element_type=F32
        )
        radial = radial.astype(BF).astype(F32)
        at = k * GROUPS + g
        left[pl.ds(at, 48, stride=PITCH), :] = radial[:, :128]
        right[pl.ds(at, 48, stride=PITCH), :] = radial[:, 128:]
        return carry

    lax.fori_loop(0, GROUPS, group, 0, unroll=True)

    @pl.when(k == STEPS - 1)
    def _():
        fetch.wait()
        slot = lax.broadcasted_iota(jnp.int32, (64, SPAN), 1)
        low_slot = slot < GROUPS * n_low
        near = lax.broadcasted_iota(jnp.int32, (32, 128), 1) < 64
        even_row = (lax.broadcasted_iota(jnp.int32, (32, 128), 0) & 1) == 0

        def order(i, carry):
            first = angular_ref[i, 0:64, 0:SPAN]
            second = angular_ref[i, 64:128, 0:SPAN]
            zero = jnp.zeros_like(first)
            first = jnp.concatenate(
                [jnp.where(low_slot, first, zero), jnp.where(low_slot, zero, first)], axis=0
            )
            second = jnp.concatenate(
                [jnp.where(low_slot, second, zero), jnp.where(low_slot, zero, second)], axis=0
            )
            folded = [[None, None], [None, None]]
            for c in range(2):
                at = pl.multiple_of((c * PAIR_DEV + i) * PITCH, 8)
                one = jnp.dot(first, left[pl.ds(at, SPAN), :].astype(BF), preferred_element_type=F32)
                two = jnp.dot(second, right[pl.ds(at, SPAN), :].astype(BF), preferred_element_type=F32)
                both = one + two
                for seg in range(2):
                    total = jnp.where(near, both[64 * seg : 64 * seg + 32], both[64 * seg + 32 : 64 * seg + 64])
                    other = pltpu.roll(total, 64, 1)
                    sign = jnp.where((i + seg) % 2 == 0, 1.0, -1.0)
                    folded[c][seg] = jnp.where(near, total + other, (other - total) * sign)
            for seg in range(2):
                scale = twist_ref[3 * e + 2, seg * PAIR_DEV + i]
                cos = jnp.where(even_row, twist_ref[3 * e, seg * PAIR_DEV + i], scale)
                sin = jnp.where(even_row, twist_ref[3 * e + 1, seg * PAIR_DEV + i], 0.0)
                real, imag = folded[0][seg], folded[1][seg]
                turned[pl.ds(seg * 48 + i, 32, stride=96), :] = real * cos + imag * sin
                turned[pl.ds(seg * 48 + PAIR_DEV + i, 32, stride=96), :] = imag * cos - real * sin
            return carry

        lax.fori_loop(0, PAIR_DEV, order, 0, unroll=8)

        def pair(q, carry):
            rows = [
                jnp.transpose(turned[pl.ds(pl.multiple_of((2 * q + d) * 96, 8), 96), :])
                for d in range(2)
            ]
            for side, order in ((0, rows), (1, rows[::-1])):
                packed = jnp.concatenate(
                    [x[64 * side + 32 * f : 64 * side + 32 * f + 32] for x in order for f in range(2)],
                    axis=1,
                )
                for owner in range(8):
                    value = packed[4 * owner : 4 * owner + 4].astype(BF)
                    out_ref[owner, 31 - q if side else q] = value
            return carry

        lax.fori_loop(0, 16, pair, 0, unroll=4)


def cycle_sums(e, twist, coeffs, gathered, angular):
    return pl.pallas_call(
        sums_kernel,
        out_shape=jax.ShapeDtypeStruct((8, 32, 4, 384), BF),
        grid_spec=pltpu.PrefetchScalarGridSpec(
            num_scalar_prefetch=2,
            grid=(STEPS,),
            in_specs=[
                pl.BlockSpec((1, GROUPS, 48, 128), lambda k, s, t: (k, 0, 0, 0)),
                *[pl.BlockSpec(memory_space=pl.ANY)] * 9,
            ],
            out_specs=pl.BlockSpec((8, 32, 4, 384), lambda k, s, t: (0, 0, 0, 0)),
            scratch_shapes=[
                pltpu.VMEM((48 * PITCH, 128), F32),
                pltpu.VMEM((48 * PITCH, 128), F32),
                pltpu.VMEM((32 * 96, 128), F32),
                pltpu.VMEM((L // 4, 64, 128), BF),
                pltpu.VMEM((PAIR_DEV, 128, KPAD), BF),
                pltpu.SemaphoreType.DMA((32,)),
                pltpu.SemaphoreType.DMA,
            ],
        ),
        compiler_params=pltpu.CompilerParams(vmem_limit_bytes=56 * 2**20),
        name="cycle_sums",
    )(e, twist, coeffs, *gathered, angular)


SOURCES_STEP = 8


def pixels_kernel(in_ref, basis_ref, dens_ref, disp_ref, total):
    step = pl.program_id(0)
    col = lax.broadcasted_iota(jnp.int32, (16, 96), 1)
    order = col % PAIR_DEV
    odd = (order + jnp.where(col >= 48, 1, 0)) % 2 == 1
    acc = None
    for source in range(SOURCES_STEP):
        value = in_ref[0, source].astype(F32)
        for radial in range(1, 8):
            value = value + in_ref[radial, source].astype(F32)
        value = jnp.concatenate([value[:, 96 * part : 96 * part + 96] for part in range(4)], axis=0)
        top = value.astype(BF).astype(F32)
        rest = value - top
        rows = jnp.concatenate(
            [
                jnp.where(odd, 0.0, top),
                jnp.where(odd, top, 0.0),
                jnp.where(odd, 0.0, rest),
                jnp.where(odd, rest, 0.0),
            ],
            axis=0,
        ).astype(BF)
        part = jnp.dot(rows, basis_ref[source], preferred_element_type=F32)
        part = part[0:32] + part[32:64]
        acc = part if acc is None else acc + part

    @pl.when(step == 0)
    def _():
        total[...] = acc

    @pl.when(step > 0)
    def _():
        total[...] += acc

    @pl.when(step == pl.num_programs(0) - 1)
    def _():
        even, odd_part = total[0:16], total[16:32]
        near, far = even + odd_part, even - odd_part
        for cycle in range(2):
            for shell in range(4):
                at = cycle * 8 + shell
                for ref, row in ((dens_ref, at), (disp_ref, at + 4)):
                    ref[shell, cycle : cycle + 1, 0:HALF_PIX] = near[row : row + 1]
                    ref[shell, cycle : cycle + 1, HALF_PIX:] = far[row : row + 1]


def pixel_basis():
    source = np.arange(32)[:, None, None]
    i = np.arange(PAIR_DEV)[None, None, :]
    low = PAIR_DEV * source + i
    orders = np.concatenate([low, L - 1 - low], axis=1)
    phase = (orders[..., None] * (np.arange(HALF_PIX) + 1)) % 2048
    angle = 2.0 * math.pi / 2048 * phase
    basis = np.stack([np.cos(angle), -np.sin(angle)], axis=2)
    return basis.reshape(32, 96, HALF_PIX).astype(jnp.bfloat16)


def pixels(received):
    out = jax.ShapeDtypeStruct((4, 2, 2 * HALF_PIX), F32)
    spec = pl.BlockSpec((4, 2, 2 * HALF_PIX), lambda k: (0, 0, 0))
    return pl.pallas_call(
        pixels_kernel,
        out_shape=(out, out),
        grid=(32 // SOURCES_STEP,),
        in_specs=[
            pl.BlockSpec((8, SOURCES_STEP, 4, 384), lambda k: (0, k, 0, 0)),
            pl.BlockSpec((SOURCES_STEP, 96, HALF_PIX), lambda k: (k, 0, 0)),
        ],
        out_specs=(spec, spec),
        scratch_shapes=[pltpu.VMEM((32, HALF_PIX), F32)],
        compiler_params=pltpu.CompilerParams(vmem_limit_bytes=48 * 2**20),
        name="pixels",
    )(received, jnp.asarray(pixel_basis()))


def table_kernel(r_ref, bessel_ref, counts_ref, out_ref, stage, grouped):
    width = bessel_ref.shape[3]
    mode = lax.broadcasted_iota(jnp.int32, (MODES_DEV, width), 0) + MODES_DEV * r_ref[0]
    live = mode < counts_ref[...]
    lane = lax.broadcasted_iota(jnp.int32, (8, 128), 1)
    for owner in range(8):
        for f in range(2):
            for shell in range(4):
                row = (f * 32 + owner * 4 + shell) * ROW_PITCH
                value = bessel_ref[f, owner * 4 + shell].astype(F32)
                stage[row : row + MODES_DEV, 0:width] = jnp.where(live, value, 0.0)

    def one(owner, carry):
        parts = [
            stage[pl.ds(owner * 8 * ROW_PITCH + n, 8, stride=ROW_PITCH), :] for n in range(MODES_DEV)
        ]
        parts = butterfly(parts, lane)
        for g in range(width // 4):
            grouped[g, pl.ds(pl.multiple_of(owner * 8, 8), 8), :] = parts[g]
        return carry

    lax.fori_loop(0, 8, one, 0, unroll=2)
    for g in range(width // 4):
        out_ref[g] = grouped[g].astype(BF)


def radial_table(bessel, mode_counts):
    width = bessel.shape[3]
    counts = lax.dynamic_slice_in_dim(mode_counts, lax.axis_index("ell") * width, width)
    return pl.pallas_call(
        table_kernel,
        out_shape=jax.ShapeDtypeStruct((width // 4, 64, 128), BF),
        grid_spec=pltpu.PrefetchScalarGridSpec(
            num_scalar_prefetch=1,
            grid=(1,),
            in_specs=[
                pl.BlockSpec(bessel.shape, lambda k, s: (0, 0, 0, 0)),
                pl.BlockSpec((1, width), lambda k, s: (0, 0)),
            ],
            out_specs=pl.BlockSpec((width // 4, 64, 128), lambda k, s: (0, 0, 0)),
            scratch_shapes=[
                pltpu.VMEM((64 * ROW_PITCH, 128), F32),
                pltpu.VMEM((width // 4, 64, 128), F32),
            ],
        ),
        compiler_params=pltpu.CompilerParams(vmem_limit_bytes=32 * 2**20),
        name="radial_table",
    )(lax.axis_index("rad").reshape(1).astype(jnp.int32), bessel, counts.reshape(1, width))


def ring_shift(value, shift, first):
    pairs = []
    for e in range(32):
        core, x, y = e % 2, (e // 2) % 4, e // 8
        if (core == 0) == first:
            x = (x + shift) % 4
        else:
            y = (y + shift) % 4
        pairs.append((e, (y * 4 + x) * 2 + core))
    return lax.ppermute(value, "ell", pairs)


def other_core(value):
    return lax.ppermute(value, "ell", [(e, e ^ 1) for e in range(32)])


def twist_table():
    low = np.arange(L // 2).reshape(32, PAIR_DEV)
    orders = np.concatenate([low, L - 1 - low], axis=1)
    weight = np.where(orders == 0, 1.0, 2.0)
    angle = 2.0 * math.pi / 4096 * orders
    return np.stack([weight * np.cos(angle), weight * np.sin(angle), weight], axis=1).reshape(96, 48).astype(np.float32)


def local(coefficients, legendre, bessel, mode_counts):
    e = lax.axis_index("ell")
    e_arr = e.reshape(1).astype(jnp.int32)
    twist = jnp.asarray(twist_table())
    table = radial_table(bessel, mode_counts)
    moved = [ring_shift(table, shift, True) for shift in SHIFTS[1:]]
    angular = angular_blocks(e_arr, legendre)
    angular, *moved = lax.optimization_barrier((angular, *moved))
    own = jnp.concatenate([table, *moved], axis=0)
    far = [ring_shift(own, shift, False) for shift in SHIFTS[1:]]
    e_late, own = lax.optimization_barrier((e_arr, own))
    coeffs = coeff_blocks(e_late, coefficients)
    coeffs, *far = lax.optimization_barrier((coeffs, *far))
    mine = [own, *far]
    gathered = mine + [other_core(value) for value in mine]
    sums = cycle_sums(e_arr, twist, coeffs, gathered, angular)
    received = lax.all_to_all(
        sums.reshape(256, 4, 384), ("rad", "ell"), split_axis=0, concat_axis=0, tiled=True
    )
    return pixels(received.reshape(8, 32, 4, 384))


def solution(mesh):
    in_specs = (P(None, "rad", "ell", None), P(None, "ell", None), P(None, None, "rad", "ell"), P())
    out_specs = (P("rad", "ell", None), P("rad", "ell", None))
    return jax.shard_map(local, mesh=mesh, in_specs=in_specs, out_specs=out_specs, check_vma=False)
```

```python
import functools
import math

import jax
import jax.numpy as jnp
import numpy as np
from jax import lax
from jax.experimental import pallas as pl
from jax.experimental.pallas import tpu as pltpu
from jax.sharding import PartitionSpec as P

L = 1536
HALF_PIX = 1024
PAIR_DEV = 24
MODES_DEV = 32
STEPS = 14
GROUPS = 32
SPAN = STEPS * GROUPS
PITCH = SPAN + 8
KPAD = 512
ROW_PITCH = 40
PIECE = 12
SHIFTS = (0, 1, -1, 2)
BF = jnp.bfloat16
F32 = jnp.float32


def step_info(k, e):
    p0 = PAIR_DEV * e
    n_low = 12 - p0 // 128
    first_high = (L - PAIR_DEV - p0) // 128
    is_low = k < n_low
    high_block = k - n_low + first_high
    return p0, n_low, is_low, high_block


def window_low(k, e):
    _, _, is_low, high_block = step_info(k, e)
    return jnp.where(is_low, jnp.maximum(k - 1, 0), jnp.minimum(high_block, 11))


def window_high(k, e):
    _, _, is_low, high_block = step_info(k, e)
    return jnp.where(is_low, k, jnp.minimum(high_block, 11) + 1)


def exchange(parts, lane):
    parts = [parts[-g % 32] for g in range(32)]
    for bit in range(5):
        upper = (lane & (4 << bit)) != 0
        parts = [jnp.where(upper, parts[(g - (1 << bit)) % 32], parts[g]) for g in range(32)]
    return [pltpu.roll(parts[g], -4 * g % 128, 1) if g else parts[g] for g in range(32)]


def coeff_kernel(e_ref, first_ref, second_ref, out_ref):
    k = pl.program_id(0)
    _, _, is_low, _ = step_info(k, e_ref[0])
    lane8 = lax.broadcasted_iota(jnp.int32, (8, 128), 1)
    row8 = lax.broadcasted_iota(jnp.int32, (8, 128), 0)
    lane = lax.broadcasted_iota(jnp.int32, (16, 128), 1)

    def run(shifted):
        for tile in range(3):
            parts = []
            for n in range(MODES_DEV):
                halves = []
                for half in range(2):
                    c, sub = divmod(2 * tile + half, 3)
                    a = first_ref[c, n].astype(F32)[8 * sub : 8 * sub + 8]
                    b = second_ref[c, n].astype(F32)[8 * sub : 8 * sub + 8]
                    halves.append(shifted(a, b, sub, n))
                parts.append(jnp.concatenate(halves, axis=0).astype(BF))
            parts = exchange(parts, lane)
            for g in range(GROUPS):
                out_ref[0, g, 16 * tile : 16 * tile + 16, :] = parts[g]

    @pl.when(is_low)
    def _():
        def shifted(a, b, sub, n):
            mixed = jnp.where(lane8 < 128 - 8 * sub - row8, b, a)
            base = (8 * sub + 4 * n) % 128
            if base > 120:
                return pltpu.roll(pltpu.roll(mixed, base - 64, 1, stride=1, stride_axis=0), 64, 1)
            return pltpu.roll(mixed, base, 1, stride=1, stride_axis=0)

        run(shifted)

    @pl.when(jnp.logical_not(is_low))
    def _():
        def shifted(a, b, sub, n):
            return pltpu.roll(jnp.where(lane8 >= 1, a, b), (127 + 4 * n) % 128, 1)

        run(shifted)


def coeff_blocks(e, coefficients):
    block = (2, MODES_DEV, PAIR_DEV, 128)
    return pl.pallas_call(
        coeff_kernel,
        out_shape=jax.ShapeDtypeStruct((STEPS, GROUPS, 2 * PAIR_DEV, 128), BF),
        grid_spec=pltpu.PrefetchScalarGridSpec(
            num_scalar_prefetch=1,
            grid=(STEPS,),
            in_specs=[
                pl.BlockSpec(block, lambda k, s: (0, 0, 0, window_low(k, s[0]))),
                pl.BlockSpec(block, lambda k, s: (0, 0, 0, window_high(k, s[0]))),
            ],
            out_specs=pl.BlockSpec((1, GROUPS, 2 * PAIR_DEV, 128), lambda k, s: (k, 0, 0, 0)),
        ),
        compiler_params=pltpu.CompilerParams(vmem_limit_bytes=48 * 2**20),
        name="coeff_blocks",
    )(e, coefficients, coefficients)


def angular_kernel(e_ref, first_ref, second_ref, out_ref, stage, wide, pick_ref):
    k = pl.program_id(0)
    e = e_ref[0]
    p0, _, is_low, high_block = step_info(k, e)
    quarter = k % 4

    @pl.when(k == 0)
    def _():
        slot = lax.broadcasted_iota(jnp.int32, (512, 128), 0)
        column = lax.broadcasted_iota(jnp.int32, (512, 128), 1)
        group = 32 * (slot >> 7) + ((slot & 127) >> 2)
        for j in range(4):
            hit = (column == group) & ((slot & 3) == j)
            pick_ref[:, 128 * j : 128 * j + 128] = jnp.where(hit, 1.0, 0.0).astype(BF)

    lane = lax.broadcasted_iota(jnp.int32, (PAIR_DEV, 128), 1)
    row = lax.broadcasted_iota(jnp.int32, (PAIR_DEV, 128), 0)

    def run(shifted, keep):
        for r in range(32):
            value = shifted(first_ref[r].astype(F32), second_ref[r].astype(F32))
            value = jnp.where(keep, value, 0.0)
            stage[pl.ds(r, PAIR_DEV, stride=ROW_PITCH), :] = value

    @pl.when(jnp.logical_and(is_low, k < STEPS))
    def _():
        def shifted(a, b):
            mixed = jnp.where(lane < 128 - row, b, a)
            return pltpu.roll(mixed, 0, 1, stride=1, stride_axis=0)

        offset = 128 * k + lane
        run(shifted, (offset >= row) & (offset < L - p0))

    @pl.when(jnp.logical_and(jnp.logical_not(is_low), k < STEPS))
    def _():
        def shifted(a, b):
            return pltpu.roll(jnp.where(lane >= 1, a, b), 127, 1)

        degree = 128 * high_block + lane
        run(shifted, (degree >= L - 1 - p0 - row) & (degree < L))

    @pl.when(k >= STEPS)
    def _():
        stage[...] = jnp.zeros_like(stage)

    for q in range(4):
        @pl.when(quarter == q)
        def _():
            for i in range(PAIR_DEV):
                value = stage[ROW_PITCH * i : ROW_PITCH * i + 32, :].astype(BF)
                wide[32 * i : 32 * i + 32, 128 * q : 128 * q + 128] = value

    @pl.when(quarter == 3)
    def _():
        for j in range(4):
            picked = jnp.dot(
                wide[...], pick_ref[:, 128 * j : 128 * j + 128], preferred_element_type=F32
            )
            for i in range(PAIR_DEV):
                out_ref[i, 32 * j : 32 * j + 32, :] = picked[32 * i : 32 * i + 32].astype(BF)


def angular_blocks(e, legendre):
    block = (32, PAIR_DEV, 128)
    return pl.pallas_call(
        angular_kernel,
        out_shape=jax.ShapeDtypeStruct((PAIR_DEV, 128, KPAD), BF),
        grid_spec=pltpu.PrefetchScalarGridSpec(
            num_scalar_prefetch=1,
            grid=(16,),
            in_specs=[
                pl.BlockSpec(block, lambda k, s: (0, 0, window_low(jnp.minimum(k, STEPS - 1), s[0]))),
                pl.BlockSpec(block, lambda k, s: (0, 0, window_high(jnp.minimum(k, STEPS - 1), s[0]))),
            ],
            out_specs=pl.BlockSpec((PAIR_DEV, 128, 128), lambda k, s: (0, 0, k // 4)),
            scratch_shapes=[pltpu.VMEM((PAIR_DEV * ROW_PITCH, 128), F32), pltpu.VMEM((PAIR_DEV * 32, 512), BF), pltpu.VMEM((512, 512), BF)],
        ),
        compiler_params=pltpu.CompilerParams(vmem_limit_bytes=48 * 2**20),
        name="angular_blocks",
    )(e, legendre, legendre)


def table_first(k, e):
    p0, _, is_low, high_block = step_info(k, e)
    return jnp.where(is_low, p0 // 4 + GROUPS * k, GROUPS * jnp.minimum(high_block, 11))


def piece_owner(e, other_core, second, first):
    core = (e + other_core) % 2
    x, y = (e // 2) % 4, e // 8
    along_x = jnp.where(core == 0, SHIFTS[first], SHIFTS[second])
    along_y = jnp.where(core == 0, SHIFTS[second], SHIFTS[first])
    return (((y + 4 - along_y) % 4) * 4 + (x + 4 - along_x) % 4) * 2 + core


def sums_kernel(e_ref, twist_ref, coeff_ref, *refs):
    gathered, (angular_hbm, out_ref, left, right, turned, table_ref, angular_ref, sems, sem) = refs[:8], refs[8:]
    k = pl.program_id(0)
    e = e_ref[0]
    p0, n_low, _, _ = step_info(k, e)
    base = table_first(k, e)
    fetch = pltpu.make_async_copy(angular_hbm, angular_ref, sem)
    first_piece = p0 // 4 // PIECE

    @pl.when(k == 0)
    def _():
        for buffer in range(8):
            other_core, second = divmod(buffer, 4)
            for first in range(4):
                owner = piece_owner(e, other_core, second, first)

                @pl.when(owner >= first_piece)
                def _():
                    pltpu.make_async_copy(
                        gathered[buffer].at[pl.ds(first * PIECE, PIECE)],
                        table_ref.at[pl.ds(owner * PIECE, PIECE)],
                        sems.at[owner],
                    ).start()

        fetch.start()

    last_group = L // 4 - 1
    wait_from = jnp.where(
        k == 0, first_piece, jnp.minimum(p0 // 4 + GROUPS * k - 1, last_group) // PIECE + 1
    )
    wait_to = jnp.minimum(p0 // 4 + GROUPS * k + GROUPS - 1, last_group) // PIECE + 1

    def arrive(piece, carry):
        pltpu.make_async_copy(
            gathered[0].at[pl.ds(0, PIECE)], table_ref.at[pl.ds(piece * PIECE, PIECE)], sems.at[piece]
        ).wait()
        return carry

    lax.fori_loop(wait_from, wait_to, arrive, 0)

    lane = lax.broadcasted_iota(jnp.int32, (64, 128), 1)
    slots = [(lane & 3) == j for j in range(4)]

    def group(g, carry):
        table = table_ref[jnp.minimum(base + g, last_group)]
        weights = jnp.concatenate(
            [jnp.where(slots[j], table, jnp.zeros_like(table)) for j in range(4)], axis=0
        )
        radial = lax.dot_general(
            coeff_ref[0, g], weights, (((1,), (1,)), ((), ())), preferred_element_type=F32
        )
        radial = radial.astype(BF).astype(F32)
        at = k * GROUPS + g
        left[pl.ds(at, 48, stride=PITCH), :] = radial[:, :128]
        right[pl.ds(at, 48, stride=PITCH), :] = radial[:, 128:]
        return carry

    lax.fori_loop(0, GROUPS, group, 0, unroll=True)

    @pl.when(k == STEPS - 1)
    def _():
        fetch.wait()
        slot = lax.broadcasted_iota(jnp.int32, (64, SPAN), 1)
        low_slot = slot < GROUPS * n_low
        near = lax.broadcasted_iota(jnp.int32, (32, 128), 1) < 64
        even_row = (lax.broadcasted_iota(jnp.int32, (32, 128), 0) & 1) == 0

        def order(i, carry):
            first = angular_ref[i, 0:64, 0:SPAN]
            second = angular_ref[i, 64:128, 0:SPAN]
            zero = jnp.zeros_like(first)
            first = jnp.concatenate(
                [jnp.where(low_slot, first, zero), jnp.where(low_slot, zero, first)], axis=0
            )
            second = jnp.concatenate(
                [jnp.where(low_slot, second, zero), jnp.where(low_slot, zero, second)], axis=0
            )
            folded = [[None, None], [None, None]]
            for c in range(2):
                at = pl.multiple_of((c * PAIR_DEV + i) * PITCH, 8)
                one = jnp.dot(first, left[pl.ds(at, SPAN), :].astype(BF), preferred_element_type=F32)
                two = jnp.dot(second, right[pl.ds(at, SPAN), :].astype(BF), preferred_element_type=F32)
                both = one + two
                for seg in range(2):
                    total = jnp.where(near, both[64 * seg : 64 * seg + 32], both[64 * seg + 32 : 64 * seg + 64])
                    other = pltpu.roll(total, 64, 1)
                    sign = jnp.where((i + seg) % 2 == 0, 1.0, -1.0)
                    folded[c][seg] = jnp.where(near, total + other, (other - total) * sign)
            for seg in range(2):
                scale = twist_ref[3 * e + 2, seg * PAIR_DEV + i]
                cos = jnp.where(even_row, twist_ref[3 * e, seg * PAIR_DEV + i], scale)
                sin = jnp.where(even_row, twist_ref[3 * e + 1, seg * PAIR_DEV + i], 0.0)
                real, imag = folded[0][seg], folded[1][seg]
                turned[pl.ds(seg * 48 + i, 32, stride=96), :] = real * cos + imag * sin
                turned[pl.ds(seg * 48 + PAIR_DEV + i, 32, stride=96), :] = imag * cos - real * sin
            return carry

        lax.fori_loop(0, PAIR_DEV, order, 0, unroll=8)

        def pair(q, carry):
            rows = [
                jnp.transpose(turned[pl.ds(pl.multiple_of((2 * q + d) * 96, 8), 96), :])
                for d in range(2)
            ]
            for side, order in ((0, rows), (1, rows[::-1])):
                packed = jnp.concatenate(
                    [x[64 * side + 32 * f : 64 * side + 32 * f + 32] for x in order for f in range(2)],
                    axis=1,
                )
                for owner in range(8):
                    value = packed[4 * owner : 4 * owner + 4].astype(BF)
                    out_ref[owner, 31 - q if side else q] = value
            return carry

        lax.fori_loop(0, 16, pair, 0, unroll=4)


def cycle_sums(e, twist, coeffs, gathered, angular):
    return pl.pallas_call(
        sums_kernel,
        out_shape=jax.ShapeDtypeStruct((8, 32, 4, 384), BF),
        grid_spec=pltpu.PrefetchScalarGridSpec(
            num_scalar_prefetch=2,
            grid=(STEPS,),
            in_specs=[
                pl.BlockSpec((1, GROUPS, 48, 128), lambda k, s, t: (k, 0, 0, 0)),
                *[pl.BlockSpec(memory_space=pl.ANY)] * 9,
            ],
            out_specs=pl.BlockSpec((8, 32, 4, 384), lambda k, s, t: (0, 0, 0, 0)),
            scratch_shapes=[
                pltpu.VMEM((48 * PITCH, 128), F32),
                pltpu.VMEM((48 * PITCH, 128), F32),
                pltpu.VMEM((32 * 96, 128), F32),
                pltpu.VMEM((L // 4, 64, 128), BF),
                pltpu.VMEM((PAIR_DEV, 128, KPAD), BF),
                pltpu.SemaphoreType.DMA((32,)),
                pltpu.SemaphoreType.DMA,
            ],
        ),
        compiler_params=pltpu.CompilerParams(vmem_limit_bytes=56 * 2**20),
        name="cycle_sums",
    )(e, twist, coeffs, *gathered, angular)


SOURCES_STEP = 16


def pixels_kernel(in_ref, basis_ref, dens_ref, disp_ref, total):
    step = pl.program_id(0)
    col = lax.broadcasted_iota(jnp.int32, (16, 96), 1)
    order = col % PAIR_DEV
    odd = (order + jnp.where(col >= 48, 1, 0)) % 2 == 1
    acc = None
    for source in range(SOURCES_STEP):
        value = in_ref[0, source].astype(F32)
        for radial in range(1, 8):
            value = value + in_ref[radial, source].astype(F32)
        value = jnp.concatenate([value[:, 96 * part : 96 * part + 96] for part in range(4)], axis=0)
        top = value.astype(BF).astype(F32)
        rest = value - top
        rows = jnp.concatenate(
            [
                jnp.where(odd, 0.0, top),
                jnp.where(odd, top, 0.0),
                jnp.where(odd, 0.0, rest),
                jnp.where(odd, rest, 0.0),
            ],
            axis=0,
        ).astype(BF)
        part = jnp.dot(rows, basis_ref[source], preferred_element_type=F32)
        part = part[0:32] + part[32:64]
        acc = part if acc is None else acc + part

    @pl.when(step == 0)
    def _():
        total[...] = acc

    @pl.when(step > 0)
    def _():
        total[...] += acc

    @pl.when(step == pl.num_programs(0) - 1)
    def _():
        even, odd_part = total[0:16], total[16:32]
        near, far = even + odd_part, even - odd_part
        for cycle in range(2):
            for shell in range(4):
                at = cycle * 8 + shell
                for ref, row in ((dens_ref, at), (disp_ref, at + 4)):
                    ref[shell, cycle : cycle + 1, 0:HALF_PIX] = near[row : row + 1]
                    ref[shell, cycle : cycle + 1, HALF_PIX:] = far[row : row + 1]


def pixel_basis():
    source = np.arange(32)[:, None, None]
    i = np.arange(PAIR_DEV)[None, None, :]
    low = PAIR_DEV * source + i
    orders = np.concatenate([low, L - 1 - low], axis=1)
    phase = (orders[..., None] * (np.arange(HALF_PIX) + 1)) % 2048
    angle = 2.0 * math.pi / 2048 * phase
    basis = np.stack([np.cos(angle), -np.sin(angle)], axis=2)
    return basis.reshape(32, 96, HALF_PIX).astype(jnp.bfloat16)


def pixels(received):
    out = jax.ShapeDtypeStruct((4, 2, 2 * HALF_PIX), F32)
    spec = pl.BlockSpec((4, 2, 2 * HALF_PIX), lambda k: (0, 0, 0))
    return pl.pallas_call(
        pixels_kernel,
        out_shape=(out, out),
        grid=(32 // SOURCES_STEP,),
        in_specs=[
            pl.BlockSpec((8, SOURCES_STEP, 4, 384), lambda k: (0, k, 0, 0)),
            pl.BlockSpec((SOURCES_STEP, 96, HALF_PIX), lambda k: (k, 0, 0)),
        ],
        out_specs=(spec, spec),
        scratch_shapes=[pltpu.VMEM((32, HALF_PIX), F32)],
        compiler_params=pltpu.CompilerParams(vmem_limit_bytes=48 * 2**20),
        name="pixels",
    )(received, jnp.asarray(pixel_basis()))


def table_kernel(r_ref, bessel_ref, counts_ref, out_ref, stage, grouped):
    width = bessel_ref.shape[3]
    mode = lax.broadcasted_iota(jnp.int32, (MODES_DEV, width), 0) + MODES_DEV * r_ref[0]
    live = mode < counts_ref[...]
    lane = lax.broadcasted_iota(jnp.int32, (8, 128), 1)
    for owner in range(8):
        for f in range(2):
            for shell in range(4):
                row = (f * 32 + owner * 4 + shell) * ROW_PITCH
                value = bessel_ref[f, owner * 4 + shell].astype(F32)
                stage[row : row + MODES_DEV, 0:width] = jnp.where(live, value, 0.0)

    def one(owner, carry):
        parts = [
            stage[pl.ds(owner * 8 * ROW_PITCH + n, 8, stride=ROW_PITCH), :] for n in range(MODES_DEV)
        ]
        parts = exchange([pltpu.roll(x, 4 * n, 1) if n else x for n, x in enumerate(parts)], lane)
        for g in range(width // 4):
            grouped[g, pl.ds(pl.multiple_of(owner * 8, 8), 8), :] = parts[g]
        return carry

    lax.fori_loop(0, 8, one, 0, unroll=2)
    for g in range(width // 4):
        out_ref[g] = grouped[g].astype(BF)


def radial_table(bessel, mode_counts):
    width = bessel.shape[3]
    counts = lax.dynamic_slice_in_dim(mode_counts, lax.axis_index("ell") * width, width)
    return pl.pallas_call(
        table_kernel,
        out_shape=jax.ShapeDtypeStruct((width // 4, 64, 128), BF),
        grid_spec=pltpu.PrefetchScalarGridSpec(
            num_scalar_prefetch=1,
            grid=(1,),
            in_specs=[
                pl.BlockSpec(bessel.shape, lambda k, s: (0, 0, 0, 0)),
                pl.BlockSpec((1, width), lambda k, s: (0, 0)),
            ],
            out_specs=pl.BlockSpec((width // 4, 64, 128), lambda k, s: (0, 0, 0)),
            scratch_shapes=[
                pltpu.VMEM((64 * ROW_PITCH, 128), F32),
                pltpu.VMEM((width // 4, 64, 128), F32),
            ],
        ),
        compiler_params=pltpu.CompilerParams(vmem_limit_bytes=32 * 2**20),
        name="radial_table",
    )(lax.axis_index("rad").reshape(1).astype(jnp.int32), bessel, counts.reshape(1, width))


def ring_shift(value, shift, first):
    pairs = []
    for e in range(32):
        core, x, y = e % 2, (e // 2) % 4, e // 8
        if (core == 0) == first:
            x = (x + shift) % 4
        else:
            y = (y + shift) % 4
        pairs.append((e, (y * 4 + x) * 2 + core))
    return lax.ppermute(value, "ell", pairs)


def other_core(value):
    return lax.ppermute(value, "ell", [(e, e ^ 1) for e in range(32)])


def twist_table():
    low = np.arange(L // 2).reshape(32, PAIR_DEV)
    orders = np.concatenate([low, L - 1 - low], axis=1)
    weight = np.where(orders == 0, 1.0, 2.0)
    angle = 2.0 * math.pi / 4096 * orders
    return np.stack([weight * np.cos(angle), weight * np.sin(angle), weight], axis=1).reshape(96, 48).astype(np.float32)


def local(coefficients, legendre, bessel, mode_counts):
    e = lax.axis_index("ell")
    e_arr = e.reshape(1).astype(jnp.int32)
    twist = jnp.asarray(twist_table())
    table = radial_table(bessel, mode_counts)
    moved = [ring_shift(table, shift, True) for shift in SHIFTS[1:]]
    angular = angular_blocks(e_arr, legendre)
    angular, *moved = lax.optimization_barrier((angular, *moved))
    own = jnp.concatenate([table, *moved], axis=0)
    far = [ring_shift(own, shift, False) for shift in SHIFTS[1:]]
    e_late, own = lax.optimization_barrier((e_arr, own))
    coeffs = coeff_blocks(e_late, coefficients)
    coeffs, *far = lax.optimization_barrier((coeffs, *far))
    mine = [own, *far]
    gathered = mine + [other_core(value) for value in mine]
    sums = cycle_sums(e_arr, twist, coeffs, gathered, angular)
    received = lax.all_to_all(
        sums.reshape(256, 4, 384), ("rad", "ell"), split_axis=0, concat_axis=0, tiled=True
    )
    return pixels(received.reshape(8, 32, 4, 384))


def solution(mesh):
    in_specs = (P(None, "rad", "ell", None), P(None, "ell", None), P(None, None, "rad", "ell"), P())
    out_specs = (P("rad", "ell", None), P("rad", "ell", None))
    return jax.shard_map(local, mesh=mesh, in_specs=in_specs, out_specs=out_specs, check_vma=False)
```

```python
import functools
import math

import jax
import jax.numpy as jnp
import numpy as np
from jax import lax
from jax.experimental import pallas as pl
from jax.experimental.pallas import tpu as pltpu
from jax.sharding import PartitionSpec as P

L = 1536
HALF_PIX = 1024
PAIR_DEV = 24
MODES_DEV = 32
STEPS = 14
GROUPS = 32
SPAN = STEPS * GROUPS
PITCH = SPAN + 8
KPAD = 512
ROW_PITCH = 40
PIECE = 12
SHIFTS = (0, 1, -1, 2)
ANGULAR_PARTS = ((0, 2), (2, 1), (3, 1))
BF = jnp.bfloat16
F32 = jnp.float32


def step_info(k, e):
    p0 = PAIR_DEV * e
    n_low = 12 - p0 // 128
    first_high = (L - PAIR_DEV - p0) // 128
    is_low = k < n_low
    high_block = k - n_low + first_high
    return p0, n_low, is_low, high_block


def window_low(k, e):
    _, _, is_low, high_block = step_info(k, e)
    return jnp.where(is_low, jnp.maximum(k - 1, 0), jnp.minimum(high_block, 11))


def window_high(k, e):
    _, _, is_low, high_block = step_info(k, e)
    return jnp.where(is_low, k, jnp.minimum(high_block, 11) + 1)


def exchange(parts, lane):
    parts = [parts[-g % 32] for g in range(32)]
    for bit in range(5):
        upper = (lane & (4 << bit)) != 0
        parts = [jnp.where(upper, parts[(g - (1 << bit)) % 32], parts[g]) for g in range(32)]
    return [pltpu.roll(parts[g], -4 * g % 128, 1) if g else parts[g] for g in range(32)]


def coeff_kernel(e_ref, first_ref, second_ref, out_ref):
    k = pl.program_id(0)
    _, _, is_low, _ = step_info(k, e_ref[0])
    lane8 = lax.broadcasted_iota(jnp.int32, (8, 128), 1)
    row8 = lax.broadcasted_iota(jnp.int32, (8, 128), 0)
    lane = lax.broadcasted_iota(jnp.int32, (16, 128), 1)

    def run(shifted):
        for tile in range(3):
            parts = []
            for n in range(MODES_DEV):
                halves = []
                for half in range(2):
                    c, sub = divmod(2 * tile + half, 3)
                    a = first_ref[c, n].astype(F32)[8 * sub : 8 * sub + 8]
                    b = second_ref[c, n].astype(F32)[8 * sub : 8 * sub + 8]
                    halves.append(shifted(a, b, sub, n))
                parts.append(jnp.concatenate(halves, axis=0).astype(BF))
            parts = exchange(parts, lane)
            for g in range(GROUPS):
                out_ref[0, g, 16 * tile : 16 * tile + 16, :] = parts[g]

    @pl.when(is_low)
    def _():
        def shifted(a, b, sub, n):
            mixed = jnp.where(lane8 < 128 - 8 * sub - row8, b, a)
            base = (8 * sub + 4 * n) % 128
            if base > 120:
                return pltpu.roll(pltpu.roll(mixed, base - 64, 1, stride=1, stride_axis=0), 64, 1)
            return pltpu.roll(mixed, base, 1, stride=1, stride_axis=0)

        run(shifted)

    @pl.when(jnp.logical_not(is_low))
    def _():
        def shifted(a, b, sub, n):
            return pltpu.roll(jnp.where(lane8 >= 1, a, b), (127 + 4 * n) % 128, 1)

        run(shifted)


def coeff_blocks(e, coefficients):
    block = (2, MODES_DEV, PAIR_DEV, 128)
    return pl.pallas_call(
        coeff_kernel,
        out_shape=jax.ShapeDtypeStruct((STEPS, GROUPS, 2 * PAIR_DEV, 128), BF),
        grid_spec=pltpu.PrefetchScalarGridSpec(
            num_scalar_prefetch=1,
            grid=(STEPS,),
            in_specs=[
                pl.BlockSpec(block, lambda k, s: (0, 0, 0, window_low(k, s[0]))),
                pl.BlockSpec(block, lambda k, s: (0, 0, 0, window_high(k, s[0]))),
            ],
            out_specs=pl.BlockSpec((1, GROUPS, 2 * PAIR_DEV, 128), lambda k, s: (k, 0, 0, 0)),
        ),
        compiler_params=pltpu.CompilerParams(vmem_limit_bytes=48 * 2**20),
        name="coeff_blocks",
    )(e, coefficients, coefficients)


def angular_kernel(start, e_ref, first_ref, second_ref, out_ref, stage, wide, pick_ref):
    k = pl.program_id(0) + start
    e = e_ref[0]
    p0, _, is_low, high_block = step_info(k, e)
    quarter = k % 4

    @pl.when(k == start)
    def _():
        slot = lax.broadcasted_iota(jnp.int32, (512, 128), 0)
        column = lax.broadcasted_iota(jnp.int32, (512, 128), 1)
        group = 32 * (slot >> 7) + ((slot & 127) >> 2)
        for j in range(4):
            hit = (column == group) & ((slot & 3) == j)
            pick_ref[:, 128 * j : 128 * j + 128] = jnp.where(hit, 1.0, 0.0).astype(BF)

    lane = lax.broadcasted_iota(jnp.int32, (PAIR_DEV, 128), 1)
    row = lax.broadcasted_iota(jnp.int32, (PAIR_DEV, 128), 0)

    def run(shifted, keep):
        for r in range(32):
            value = shifted(first_ref[r].astype(F32), second_ref[r].astype(F32))
            value = jnp.where(keep, value, 0.0)
            stage[pl.ds(r, PAIR_DEV, stride=ROW_PITCH), :] = value

    @pl.when(jnp.logical_and(is_low, k < STEPS))
    def _():
        def shifted(a, b):
            mixed = jnp.where(lane < 128 - row, b, a)
            return pltpu.roll(mixed, 0, 1, stride=1, stride_axis=0)

        offset = 128 * k + lane
        run(shifted, (offset >= row) & (offset < L - p0))

    @pl.when(jnp.logical_and(jnp.logical_not(is_low), k < STEPS))
    def _():
        def shifted(a, b):
            return pltpu.roll(jnp.where(lane >= 1, a, b), 127, 1)

        degree = 128 * high_block + lane
        run(shifted, (degree >= L - 1 - p0 - row) & (degree < L))

    @pl.when(k >= STEPS)
    def _():
        stage[...] = jnp.zeros_like(stage)

    for q in range(4):
        @pl.when(quarter == q)
        def _():
            for i in range(PAIR_DEV):
                value = stage[ROW_PITCH * i : ROW_PITCH * i + 32, :].astype(BF)
                wide[32 * i : 32 * i + 32, 128 * q : 128 * q + 128] = value

    @pl.when(quarter == 3)
    def _():
        for j in range(4):
            picked = jnp.dot(
                wide[...], pick_ref[:, 128 * j : 128 * j + 128], preferred_element_type=F32
            )
            for i in range(PAIR_DEV):
                out_ref[i, 32 * j : 32 * j + 32, :] = picked[32 * i : 32 * i + 32].astype(BF)


def angular_blocks(e, legendre, first_quad, quads):
    block = (32, PAIR_DEV, 128)
    start = 4 * first_quad
    return pl.pallas_call(
        functools.partial(angular_kernel, start),
        out_shape=jax.ShapeDtypeStruct((PAIR_DEV, 128, 128 * quads), BF),
        grid_spec=pltpu.PrefetchScalarGridSpec(
            num_scalar_prefetch=1,
            grid=(4 * quads,),
            in_specs=[
                pl.BlockSpec(
                    block, lambda k, s: (0, 0, window_low(jnp.minimum(k + start, STEPS - 1), s[0]))
                ),
                pl.BlockSpec(
                    block, lambda k, s: (0, 0, window_high(jnp.minimum(k + start, STEPS - 1), s[0]))
                ),
            ],
            out_specs=pl.BlockSpec((PAIR_DEV, 128, 128), lambda k, s: (0, 0, k // 4)),
            scratch_shapes=[
                pltpu.VMEM((PAIR_DEV * ROW_PITCH, 128), F32),
                pltpu.VMEM((PAIR_DEV * 32, 512), BF),
                pltpu.VMEM((512, 512), BF),
            ],
        ),
        compiler_params=pltpu.CompilerParams(vmem_limit_bytes=48 * 2**20),
        name="angular_blocks",
    )(e, legendre, legendre)


def table_first(k, e):
    p0, _, is_low, high_block = step_info(k, e)
    return jnp.where(is_low, p0 // 4 + GROUPS * k, GROUPS * jnp.minimum(high_block, 11))


def piece_owner(e, other_core, second, first):
    core = (e + other_core) % 2
    x, y = (e // 2) % 4, e // 8
    along_x = jnp.where(core == 0, SHIFTS[first], SHIFTS[second])
    along_y = jnp.where(core == 0, SHIFTS[second], SHIFTS[first])
    return (((y + 4 - along_y) % 4) * 4 + (x + 4 - along_x) % 4) * 2 + core


def sums_kernel(e_ref, twist_ref, coeff_ref, *refs):
    gathered, angular, refs = refs[:8], refs[8:11], refs[11:]
    out_ref, left, right, turned, table_ref, angular_ref, sems, angular_sems = refs
    k = pl.program_id(0)
    e = e_ref[0]
    p0, n_low, _, _ = step_info(k, e)
    base = table_first(k, e)
    fetches = []
    for part, (first_quad, quads) in enumerate(ANGULAR_PARTS):
        place = angular_ref.at[:, :, pl.ds(128 * first_quad, 128 * quads)]
        fetches.append(pltpu.make_async_copy(angular[part], place, angular_sems.at[part]))
    first_piece = p0 // 4 // PIECE

    @pl.when(k == 0)
    def _():
        for buffer in range(8):
            other_core, second = divmod(buffer, 4)
            for first in range(4):
                owner = piece_owner(e, other_core, second, first)

                @pl.when(owner >= first_piece)
                def _():
                    pltpu.make_async_copy(
                        gathered[buffer].at[pl.ds(first * PIECE, PIECE)],
                        table_ref.at[pl.ds(owner * PIECE, PIECE)],
                        sems.at[owner],
                    ).start()

        for fetch in fetches:
            fetch.start()

    last_group = L // 4 - 1
    wait_from = jnp.where(
        k == 0, first_piece, jnp.minimum(p0 // 4 + GROUPS * k - 1, last_group) // PIECE + 1
    )
    wait_to = jnp.minimum(p0 // 4 + GROUPS * k + GROUPS - 1, last_group) // PIECE + 1

    def arrive(piece, carry):
        pltpu.make_async_copy(
            gathered[0].at[pl.ds(0, PIECE)], table_ref.at[pl.ds(piece * PIECE, PIECE)], sems.at[piece]
        ).wait()
        return carry

    lax.fori_loop(wait_from, wait_to, arrive, 0)

    lane = lax.broadcasted_iota(jnp.int32, (64, 128), 1)
    slots = [(lane & 3) == j for j in range(4)]

    def group(g, carry):
        table = table_ref[jnp.minimum(base + g, last_group)]
        weights = jnp.concatenate(
            [jnp.where(slots[j], table, jnp.zeros_like(table)) for j in range(4)], axis=0
        )
        radial = lax.dot_general(
            coeff_ref[0, g], weights, (((1,), (1,)), ((), ())), preferred_element_type=F32
        )
        radial = radial.astype(BF).astype(F32)
        at = k * GROUPS + g
        left[pl.ds(at, 48, stride=PITCH), :] = radial[:, :128]
        right[pl.ds(at, 48, stride=PITCH), :] = radial[:, 128:]
        return carry

    lax.fori_loop(0, GROUPS, group, 0, unroll=True)

    @pl.when(k == STEPS - 1)
    def _():
        for fetch in fetches:
            fetch.wait()
        slot = lax.broadcasted_iota(jnp.int32, (64, SPAN), 1)
        low_slot = slot < GROUPS * n_low
        near = lax.broadcasted_iota(jnp.int32, (32, 128), 1) < 64
        even_row = (lax.broadcasted_iota(jnp.int32, (32, 128), 0) & 1) == 0

        def order(i, carry):
            first = angular_ref[i, 0:64, 0:SPAN]
            second = angular_ref[i, 64:128, 0:SPAN]
            zero = jnp.zeros_like(first)
            first = jnp.concatenate(
                [jnp.where(low_slot, first, zero), jnp.where(low_slot, zero, first)], axis=0
            )
            second = jnp.concatenate(
                [jnp.where(low_slot, second, zero), jnp.where(low_slot, zero, second)], axis=0
            )
            folded = [[None, None], [None, None]]
            for c in range(2):
                at = pl.multiple_of((c * PAIR_DEV + i) * PITCH, 8)
                one = jnp.dot(first, left[pl.ds(at, SPAN), :].astype(BF), preferred_element_type=F32)
                two = jnp.dot(second, right[pl.ds(at, SPAN), :].astype(BF), preferred_element_type=F32)
                both = one + two
                for seg in range(2):
                    total = jnp.where(near, both[64 * seg : 64 * seg + 32], both[64 * seg + 32 : 64 * seg + 64])
                    other = pltpu.roll(total, 64, 1)
                    sign = jnp.where((i + seg) % 2 == 0, 1.0, -1.0)
                    folded[c][seg] = jnp.where(near, total + other, (other - total) * sign)
            for seg in range(2):
                scale = twist_ref[3 * e + 2, seg * PAIR_DEV + i]
                cos = jnp.where(even_row, twist_ref[3 * e, seg * PAIR_DEV + i], scale)
                sin = jnp.where(even_row, twist_ref[3 * e + 1, seg * PAIR_DEV + i], 0.0)
                real, imag = folded[0][seg], folded[1][seg]
                turned[pl.ds(seg * 48 + i, 32, stride=96), :] = real * cos + imag * sin
                turned[pl.ds(seg * 48 + PAIR_DEV + i, 32, stride=96), :] = imag * cos - real * sin
            return carry

        lax.fori_loop(0, PAIR_DEV, order, 0, unroll=8)

        def pair(q, carry):
            rows = [
                jnp.transpose(turned[pl.ds(pl.multiple_of((2 * q + d) * 96, 8), 96), :])
                for d in range(2)
            ]
            for side, order in ((0, rows), (1, rows[::-1])):
                packed = jnp.concatenate(
                    [x[64 * side + 32 * f : 64 * side + 32 * f + 32] for x in order for f in range(2)],
                    axis=1,
                )
                for owner in range(8):
                    value = packed[4 * owner : 4 * owner + 4].astype(BF)
                    out_ref[owner, 31 - q if side else q] = value
            return carry

        lax.fori_loop(0, 16, pair, 0, unroll=4)


def cycle_sums(e, twist, coeffs, gathered, angular):
    return pl.pallas_call(
        sums_kernel,
        out_shape=jax.ShapeDtypeStruct((8, 32, 4, 384), BF),
        grid_spec=pltpu.PrefetchScalarGridSpec(
            num_scalar_prefetch=2,
            grid=(STEPS,),
            in_specs=[
                pl.BlockSpec((1, GROUPS, 48, 128), lambda k, s, t: (k, 0, 0, 0)),
                *[pl.BlockSpec(memory_space=pl.ANY)] * 11,
            ],
            out_specs=pl.BlockSpec((8, 32, 4, 384), lambda k, s, t: (0, 0, 0, 0)),
            scratch_shapes=[
                pltpu.VMEM((48 * PITCH, 128), F32),
                pltpu.VMEM((48 * PITCH, 128), F32),
                pltpu.VMEM((32 * 96, 128), F32),
                pltpu.VMEM((L // 4, 64, 128), BF),
                pltpu.VMEM((PAIR_DEV, 128, KPAD), BF),
                pltpu.SemaphoreType.DMA((32,)),
                pltpu.SemaphoreType.DMA((3,)),
            ],
        ),
        compiler_params=pltpu.CompilerParams(vmem_limit_bytes=56 * 2**20),
        name="cycle_sums",
    )(e, twist, coeffs, *gathered, *angular)


SOURCES_STEP = 16


def pixels_kernel(in_ref, basis_ref, dens_ref, disp_ref, total):
    step = pl.program_id(0)
    col = lax.broadcasted_iota(jnp.int32, (16, 96), 1)
    order = col % PAIR_DEV
    odd = (order + jnp.where(col >= 48, 1, 0)) % 2 == 1
    acc = None
    for source in range(SOURCES_STEP):
        value = in_ref[0, source].astype(F32)
        for radial in range(1, 8):
            value = value + in_ref[radial, source].astype(F32)
        value = jnp.concatenate([value[:, 96 * part : 96 * part + 96] for part in range(4)], axis=0)
        top = value.astype(BF).astype(F32)
        rest = value - top
        rows = jnp.concatenate(
            [
                jnp.where(odd, 0.0, top),
                jnp.where(odd, top, 0.0),
                jnp.where(odd, 0.0, rest),
                jnp.where(odd, rest, 0.0),
            ],
            axis=0,
        ).astype(BF)
        part = jnp.dot(rows, basis_ref[source], preferred_element_type=F32)
        part = part[0:32] + part[32:64]
        acc = part if acc is None else acc + part

    @pl.when(step == 0)
    def _():
        total[...] = acc

    @pl.when(step > 0)
    def _():
        total[...] += acc

    @pl.when(step == pl.num_programs(0) - 1)
    def _():
        even, odd_part = total[0:16], total[16:32]
        near, far = even + odd_part, even - odd_part
        for cycle in range(2):
            for shell in range(4):
                at = cycle * 8 + shell
                for ref, row in ((dens_ref, at), (disp_ref, at + 4)):
                    ref[shell, cycle : cycle + 1, 0:HALF_PIX] = near[row : row + 1]
                    ref[shell, cycle : cycle + 1, HALF_PIX:] = far[row : row + 1]


def pixel_basis():
    source = np.arange(32)[:, None, None]
    i = np.arange(PAIR_DEV)[None, None, :]
    low = PAIR_DEV * source + i
    orders = np.concatenate([low, L - 1 - low], axis=1)
    phase = (orders[..., None] * (np.arange(HALF_PIX) + 1)) % 2048
    angle = 2.0 * math.pi / 2048 * phase
    basis = np.stack([np.cos(angle), -np.sin(angle)], axis=2)
    return basis.reshape(32, 96, HALF_PIX).astype(jnp.bfloat16)


def pixels(received):
    out = jax.ShapeDtypeStruct((4, 2, 2 * HALF_PIX), F32)
    spec = pl.BlockSpec((4, 2, 2 * HALF_PIX), lambda k: (0, 0, 0))
    return pl.pallas_call(
        pixels_kernel,
        out_shape=(out, out),
        grid=(32 // SOURCES_STEP,),
        in_specs=[
            pl.BlockSpec((8, SOURCES_STEP, 4, 384), lambda k: (0, k, 0, 0)),
            pl.BlockSpec((SOURCES_STEP, 96, HALF_PIX), lambda k: (k, 0, 0)),
        ],
        out_specs=(spec, spec),
        scratch_shapes=[pltpu.VMEM((32, HALF_PIX), F32)],
        compiler_params=pltpu.CompilerParams(vmem_limit_bytes=48 * 2**20),
        name="pixels",
    )(received, jnp.asarray(pixel_basis()))


def table_kernel(r_ref, bessel_ref, counts_ref, out_ref, stage, grouped):
    width = bessel_ref.shape[3]
    mode = lax.broadcasted_iota(jnp.int32, (MODES_DEV, width), 0) + MODES_DEV * r_ref[0]
    live = mode < counts_ref[...]
    lane = lax.broadcasted_iota(jnp.int32, (8, 128), 1)
    for owner in range(8):
        for f in range(2):
            for shell in range(4):
                row = (f * 32 + owner * 4 + shell) * ROW_PITCH
                value = bessel_ref[f, owner * 4 + shell].astype(F32)
                stage[row : row + MODES_DEV, 0:width] = jnp.where(live, value, 0.0)

    def one(owner, carry):
        parts = [
            stage[pl.ds(owner * 8 * ROW_PITCH + n, 8, stride=ROW_PITCH), :] for n in range(MODES_DEV)
        ]
        parts = exchange([pltpu.roll(x, 4 * n, 1) if n else x for n, x in enumerate(parts)], lane)
        for g in range(width // 4):
            grouped[g, pl.ds(pl.multiple_of(owner * 8, 8), 8), :] = parts[g]
        return carry

    lax.fori_loop(0, 8, one, 0, unroll=2)
    for g in range(width // 4):
        out_ref[g] = grouped[g].astype(BF)


def radial_table(bessel, mode_counts):
    width = bessel.shape[3]
    counts = lax.dynamic_slice_in_dim(mode_counts, lax.axis_index("ell") * width, width)
    return pl.pallas_call(
        table_kernel,
        out_shape=jax.ShapeDtypeStruct((width // 4, 64, 128), BF),
        grid_spec=pltpu.PrefetchScalarGridSpec(
            num_scalar_prefetch=1,
            grid=(1,),
            in_specs=[
                pl.BlockSpec(bessel.shape, lambda k, s: (0, 0, 0, 0)),
                pl.BlockSpec((1, width), lambda k, s: (0, 0)),
            ],
            out_specs=pl.BlockSpec((width // 4, 64, 128), lambda k, s: (0, 0, 0)),
            scratch_shapes=[
                pltpu.VMEM((64 * ROW_PITCH, 128), F32),
                pltpu.VMEM((width // 4, 64, 128), F32),
            ],
        ),
        compiler_params=pltpu.CompilerParams(vmem_limit_bytes=32 * 2**20),
        name="radial_table",
    )(lax.axis_index("rad").reshape(1).astype(jnp.int32), bessel, counts.reshape(1, width))


def ring_shift(value, shift, first):
    pairs = []
    for e in range(32):
        core, x, y = e % 2, (e // 2) % 4, e // 8
        if (core == 0) == first:
            x = (x + shift) % 4
        else:
            y = (y + shift) % 4
        pairs.append((e, (y * 4 + x) * 2 + core))
    return lax.ppermute(value, "ell", pairs)


def other_core(value):
    return lax.ppermute(value, "ell", [(e, e ^ 1) for e in range(32)])


def twist_table():
    low = np.arange(L // 2).reshape(32, PAIR_DEV)
    orders = np.concatenate([low, L - 1 - low], axis=1)
    weight = np.where(orders == 0, 1.0, 2.0)
    angle = 2.0 * math.pi / 4096 * orders
    return np.stack([weight * np.cos(angle), weight * np.sin(angle), weight], axis=1).reshape(96, 48).astype(np.float32)


def local(coefficients, legendre, bessel, mode_counts):
    e = lax.axis_index("ell")
    e_arr = e.reshape(1).astype(jnp.int32)
    twist = jnp.asarray(twist_table())
    table = radial_table(bessel, mode_counts)
    moved = [ring_shift(table, shift, True) for shift in SHIFTS[1:]]
    early = angular_blocks(e_arr, legendre, *ANGULAR_PARTS[0])
    early, *moved = lax.optimization_barrier((early, *moved))
    own = jnp.concatenate([table, *moved], axis=0)
    far = [ring_shift(own, shift, False) for shift in SHIFTS[1:]]
    e_late, own = lax.optimization_barrier((e_arr, own))
    coeffs = coeff_blocks(e_late, coefficients)
    middle = angular_blocks(e_late, legendre, *ANGULAR_PARTS[1])
    coeffs, middle, *far = lax.optimization_barrier((coeffs, middle, *far))
    mine = [own, *far]
    theirs = [other_core(value) for value in mine]
    e_last, *far = lax.optimization_barrier((e_arr, *far))
    late = angular_blocks(e_last, legendre, *ANGULAR_PARTS[2])
    late, *theirs = lax.optimization_barrier((late, *theirs))
    gathered = mine + theirs
    angular = (early, middle, late)
    sums = cycle_sums(e_arr, twist, coeffs, gathered, angular)
    received = lax.all_to_all(
        sums.reshape(256, 4, 384), ("rad", "ell"), split_axis=0, concat_axis=0, tiled=True
    )
    return pixels(received.reshape(8, 32, 4, 384))


def solution(mesh):
    in_specs = (P(None, "rad", "ell", None), P(None, "ell", None), P(None, None, "rad", "ell"), P())
    out_specs = (P("rad", "ell", None), P("rad", "ell", None))
    return jax.shard_map(local, mesh=mesh, in_specs=in_specs, out_specs=out_specs, check_vma=False)
```

```python
import functools
import math

import jax
import jax.numpy as jnp
import numpy as np
from jax import lax
from jax.experimental import pallas as pl
from jax.experimental.pallas import tpu as pltpu
from jax.sharding import PartitionSpec as P

L = 1536
HALF_PIX = 1024
PAIR_DEV = 24
MODES_DEV = 32
STEPS = 14
GROUPS = 32
SPAN = STEPS * GROUPS
PITCH = SPAN + 8
KPAD = 512
ROW_PITCH = 40
PIECE = 6
SHIFTS = (0, 1, -1, 2)
ANGULAR_PARTS = ((0, 2), (2, 1), (3, 1))
BF = jnp.bfloat16
F32 = jnp.float32


def step_info(k, e):
    p0 = PAIR_DEV * e
    n_low = 12 - p0 // 128
    first_high = (L - PAIR_DEV - p0) // 128
    is_low = k < n_low
    high_block = k - n_low + first_high
    return p0, n_low, is_low, high_block


def window_low(k, e):
    _, _, is_low, high_block = step_info(k, e)
    return jnp.where(is_low, jnp.maximum(k - 1, 0), jnp.minimum(high_block, 11))


def window_high(k, e):
    _, _, is_low, high_block = step_info(k, e)
    return jnp.where(is_low, k, jnp.minimum(high_block, 11) + 1)


def exchange(parts, lane):
    parts = [parts[-g % 32] for g in range(32)]
    for bit in range(5):
        upper = (lane & (4 << bit)) != 0
        parts = [jnp.where(upper, parts[(g - (1 << bit)) % 32], parts[g]) for g in range(32)]
    return [pltpu.roll(parts[g], -4 * g % 128, 1) if g else parts[g] for g in range(32)]


def coeff_kernel(e_ref, first_ref, second_ref, out_ref):
    k = pl.program_id(0)
    _, _, is_low, _ = step_info(k, e_ref[0])
    lane8 = lax.broadcasted_iota(jnp.int32, (8, 128), 1)
    row8 = lax.broadcasted_iota(jnp.int32, (8, 128), 0)
    lane = lax.broadcasted_iota(jnp.int32, (16, 128), 1)

    def run(shifted):
        for tile in range(3):
            parts = []
            for n in range(MODES_DEV):
                halves = []
                for half in range(2):
                    c, sub = divmod(2 * tile + half, 3)
                    a = first_ref[c, n].astype(F32)[8 * sub : 8 * sub + 8]
                    b = second_ref[c, n].astype(F32)[8 * sub : 8 * sub + 8]
                    halves.append(shifted(a, b, sub, n))
                parts.append(jnp.concatenate(halves, axis=0).astype(BF))
            parts = exchange(parts, lane)
            for g in range(GROUPS):
                out_ref[0, g, 16 * tile : 16 * tile + 16, :] = parts[g]

    @pl.when(is_low)
    def _():
        def shifted(a, b, sub, n):
            mixed = jnp.where(lane8 < 128 - 8 * sub - row8, b, a)
            base = (8 * sub + 4 * n) % 128
            if base > 120:
                return pltpu.roll(pltpu.roll(mixed, base - 64, 1, stride=1, stride_axis=0), 64, 1)
            return pltpu.roll(mixed, base, 1, stride=1, stride_axis=0)

        run(shifted)

    @pl.when(jnp.logical_not(is_low))
    def _():
        def shifted(a, b, sub, n):
            return pltpu.roll(jnp.where(lane8 >= 1, a, b), (127 + 4 * n) % 128, 1)

        run(shifted)


def coeff_blocks(e, coefficients):
    block = (2, MODES_DEV, PAIR_DEV, 128)
    return pl.pallas_call(
        coeff_kernel,
        out_shape=jax.ShapeDtypeStruct((STEPS, GROUPS, 2 * PAIR_DEV, 128), BF),
        grid_spec=pltpu.PrefetchScalarGridSpec(
            num_scalar_prefetch=1,
            grid=(STEPS,),
            in_specs=[
                pl.BlockSpec(block, lambda k, s: (0, 0, 0, window_low(k, s[0]))),
                pl.BlockSpec(block, lambda k, s: (0, 0, 0, window_high(k, s[0]))),
            ],
            out_specs=pl.BlockSpec((1, GROUPS, 2 * PAIR_DEV, 128), lambda k, s: (k, 0, 0, 0)),
        ),
        compiler_params=pltpu.CompilerParams(vmem_limit_bytes=48 * 2**20),
        name="coeff_blocks",
    )(e, coefficients, coefficients)


def angular_kernel(start, e_ref, first_ref, second_ref, out_ref, stage, wide, pick_ref):
    k = pl.program_id(0) + start
    e = e_ref[0]
    p0, _, is_low, high_block = step_info(k, e)
    quarter = k % 4

    @pl.when(k == start)
    def _():
        slot = lax.broadcasted_iota(jnp.int32, (512, 128), 0)
        column = lax.broadcasted_iota(jnp.int32, (512, 128), 1)
        group = 32 * (slot >> 7) + ((slot & 127) >> 2)
        for j in range(4):
            hit = (column == group) & ((slot & 3) == j)
            pick_ref[:, 128 * j : 128 * j + 128] = jnp.where(hit, 1.0, 0.0).astype(BF)

    lane = lax.broadcasted_iota(jnp.int32, (PAIR_DEV, 128), 1)
    row = lax.broadcasted_iota(jnp.int32, (PAIR_DEV, 128), 0)

    def run(shifted, keep):
        for r in range(32):
            value = shifted(first_ref[r].astype(F32), second_ref[r].astype(F32))
            value = jnp.where(keep, value, 0.0)
            stage[pl.ds(r, PAIR_DEV, stride=ROW_PITCH), :] = value

    @pl.when(jnp.logical_and(is_low, k < STEPS))
    def _():
        def shifted(a, b):
            mixed = jnp.where(lane < 128 - row, b, a)
            return pltpu.roll(mixed, 0, 1, stride=1, stride_axis=0)

        offset = 128 * k + lane
        run(shifted, (offset >= row) & (offset < L - p0))

    @pl.when(jnp.logical_and(jnp.logical_not(is_low), k < STEPS))
    def _():
        def shifted(a, b):
            return pltpu.roll(jnp.where(lane >= 1, a, b), 127, 1)

        degree = 128 * high_block + lane
        run(shifted, (degree >= L - 1 - p0 - row) & (degree < L))

    @pl.when(k >= STEPS)
    def _():
        stage[...] = jnp.zeros_like(stage)

    for q in range(4):
        @pl.when(quarter == q)
        def _():
            for i in range(PAIR_DEV):
                value = stage[ROW_PITCH * i : ROW_PITCH * i + 32, :].astype(BF)
                wide[32 * i : 32 * i + 32, 128 * q : 128 * q + 128] = value

    @pl.when(quarter == 3)
    def _():
        for j in range(4):
            picked = jnp.dot(
                wide[...], pick_ref[:, 128 * j : 128 * j + 128], preferred_element_type=F32
            )
            for i in range(PAIR_DEV):
                out_ref[i, 32 * j : 32 * j + 32, :] = picked[32 * i : 32 * i + 32].astype(BF)


def angular_blocks(e, legendre, first_quad, quads):
    block = (32, PAIR_DEV, 128)
    start = 4 * first_quad
    return pl.pallas_call(
        functools.partial(angular_kernel, start),
        out_shape=jax.ShapeDtypeStruct((PAIR_DEV, 128, 128 * quads), BF),
        grid_spec=pltpu.PrefetchScalarGridSpec(
            num_scalar_prefetch=1,
            grid=(4 * quads,),
            in_specs=[
                pl.BlockSpec(
                    block, lambda k, s: (0, 0, window_low(jnp.minimum(k + start, STEPS - 1), s[0]))
                ),
                pl.BlockSpec(
                    block, lambda k, s: (0, 0, window_high(jnp.minimum(k + start, STEPS - 1), s[0]))
                ),
            ],
            out_specs=pl.BlockSpec((PAIR_DEV, 128, 128), lambda k, s: (0, 0, k // 4)),
            scratch_shapes=[
                pltpu.VMEM((PAIR_DEV * ROW_PITCH, 128), F32),
                pltpu.VMEM((PAIR_DEV * 32, 512), BF),
                pltpu.VMEM((512, 512), BF),
            ],
        ),
        compiler_params=pltpu.CompilerParams(vmem_limit_bytes=48 * 2**20),
        name="angular_blocks",
    )(e, legendre, legendre)


def table_first(k, e):
    p0, _, is_low, high_block = step_info(k, e)
    return jnp.where(is_low, p0 // 4 + GROUPS * k, GROUPS * jnp.minimum(high_block, 11))


def piece_owner(e, other_core, second, first):
    core = (e + other_core) % 2
    x, y = (e // 2) % 4, e // 8
    along_x = jnp.where(core == 0, SHIFTS[first], SHIFTS[second])
    along_y = jnp.where(core == 0, SHIFTS[second], SHIFTS[first])
    return (((y + 4 - along_y) % 4) * 4 + (x + 4 - along_x) % 4) * 2 + core


def sums_kernel(e_ref, twist_ref, coeff_ref, *refs):
    gathered, angular, refs = refs[:8], refs[8:11], refs[11:]
    out_ref, left, right, turned, table_ref, angular_ref, sems, angular_sems = refs
    k = pl.program_id(0)
    e = e_ref[0]
    p0, n_low, _, _ = step_info(k, e)
    base = table_first(k, e)
    fetches = []
    for part, (first_quad, quads) in enumerate(ANGULAR_PARTS):
        place = angular_ref.at[:, :, pl.ds(128 * first_quad, 128 * quads)]
        fetches.append(pltpu.make_async_copy(angular[part], place, angular_sems.at[part]))
    first_piece = p0 // 8 // PIECE

    @pl.when(k == 0)
    def _():
        for buffer in range(8):
            other_core, second = divmod(buffer, 4)
            for first in range(4):
                owner = piece_owner(e, other_core, second, first)

                @pl.when(owner >= first_piece)
                def _():
                    pltpu.make_async_copy(
                        gathered[buffer].at[pl.ds(first * PIECE, PIECE)],
                        table_ref.at[pl.ds(owner * PIECE, PIECE)],
                        sems.at[owner],
                    ).start()

        for fetch in fetches:
            fetch.start()

    last_group = L // 4 - 1
    wait_from = jnp.where(
        k == 0, first_piece, jnp.minimum(p0 // 4 + GROUPS * k - 1, last_group) // (2 * PIECE) + 1
    )
    wait_to = jnp.minimum(p0 // 4 + GROUPS * k + GROUPS - 1, last_group) // (2 * PIECE) + 1

    def arrive(piece, carry):
        pltpu.make_async_copy(
            gathered[0].at[pl.ds(0, PIECE)], table_ref.at[pl.ds(piece * PIECE, PIECE)], sems.at[piece]
        ).wait()
        return carry

    lax.fori_loop(wait_from, wait_to, arrive, 0)

    near_lane = lax.broadcasted_iota(jnp.int32, (128, 128), 1) < 64
    slot_row = lax.broadcasted_iota(jnp.int32, (128, 128), 0) & 3
    left_slots = slot_row == jnp.where(near_lane, 0, 1)
    right_slots = slot_row == jnp.where(near_lane, 2, 3)

    def group_pair(g, carry):
        table = table_ref[jnp.minimum(base // 2 + g, L // 8 - 1)]
        turned_table = pltpu.roll(table, 64, 1)
        zero = jnp.zeros_like(table)
        for half in range(2):
            one, two = (table, turned_table) if half == 0 else (turned_table, table)
            doubled = jnp.where(near_lane, one, two)
            weights = jnp.concatenate(
                [jnp.where(left_slots, doubled, zero), jnp.where(right_slots, doubled, zero)], axis=1
            )
            radial = jnp.dot(coeff_ref[0, 2 * g + half], weights, preferred_element_type=F32)
            radial = radial.astype(BF).astype(F32)
            at = k * GROUPS + 2 * g + half
            left[pl.ds(at, 48, stride=PITCH), :] = radial[:, :128]
            right[pl.ds(at, 48, stride=PITCH), :] = radial[:, 128:]
        return carry

    lax.fori_loop(0, GROUPS // 2, group_pair, 0, unroll=True)

    @pl.when(k == STEPS - 1)
    def _():
        for fetch in fetches:
            fetch.wait()
        slot = lax.broadcasted_iota(jnp.int32, (64, SPAN), 1)
        low_slot = slot < GROUPS * n_low
        near = lax.broadcasted_iota(jnp.int32, (32, 128), 1) < 64
        even_row = (lax.broadcasted_iota(jnp.int32, (32, 128), 0) & 1) == 0

        def order(i, carry):
            first = angular_ref[i, 0:64, 0:SPAN]
            second = angular_ref[i, 64:128, 0:SPAN]
            zero = jnp.zeros_like(first)
            first = jnp.concatenate(
                [jnp.where(low_slot, first, zero), jnp.where(low_slot, zero, first)], axis=0
            )
            second = jnp.concatenate(
                [jnp.where(low_slot, second, zero), jnp.where(low_slot, zero, second)], axis=0
            )
            folded = [[None, None], [None, None]]
            for c in range(2):
                at = pl.multiple_of((c * PAIR_DEV + i) * PITCH, 8)
                one = jnp.dot(first, left[pl.ds(at, SPAN), :].astype(BF), preferred_element_type=F32)
                two = jnp.dot(second, right[pl.ds(at, SPAN), :].astype(BF), preferred_element_type=F32)
                both = one + two
                for seg in range(2):
                    total = jnp.where(near, both[64 * seg : 64 * seg + 32], both[64 * seg + 32 : 64 * seg + 64])
                    other = pltpu.roll(total, 64, 1)
                    sign = jnp.where((i + seg) % 2 == 0, 1.0, -1.0)
                    folded[c][seg] = jnp.where(near, total + other, (other - total) * sign)
            for seg in range(2):
                scale = twist_ref[3 * e + 2, seg * PAIR_DEV + i]
                cos = jnp.where(even_row, twist_ref[3 * e, seg * PAIR_DEV + i], scale)
                sin = jnp.where(even_row, twist_ref[3 * e + 1, seg * PAIR_DEV + i], 0.0)
                real, imag = folded[0][seg], folded[1][seg]
                turned[pl.ds(seg * 48 + i, 32, stride=96), :] = real * cos + imag * sin
                turned[pl.ds(seg * 48 + PAIR_DEV + i, 32, stride=96), :] = imag * cos - real * sin
            return carry

        lax.fori_loop(0, PAIR_DEV, order, 0, unroll=8)

        def pair(q, carry):
            rows = [
                jnp.transpose(turned[pl.ds(pl.multiple_of((2 * q + d) * 96, 8), 96), :])
                for d in range(2)
            ]
            for side, order in ((0, rows), (1, rows[::-1])):
                packed = jnp.concatenate(
                    [x[64 * side + 32 * f : 64 * side + 32 * f + 32] for x in order for f in range(2)],
                    axis=1,
                )
                for owner in range(8):
                    value = packed[4 * owner : 4 * owner + 4].astype(BF)
                    out_ref[owner, 31 - q if side else q] = value
            return carry

        lax.fori_loop(0, 16, pair, 0, unroll=4)


def cycle_sums(e, twist, coeffs, gathered, angular):
    return pl.pallas_call(
        sums_kernel,
        out_shape=jax.ShapeDtypeStruct((8, 32, 4, 384), BF),
        grid_spec=pltpu.PrefetchScalarGridSpec(
            num_scalar_prefetch=2,
            grid=(STEPS,),
            in_specs=[
                pl.BlockSpec((1, GROUPS, 48, 128), lambda k, s, t: (k, 0, 0, 0)),
                *[pl.BlockSpec(memory_space=pl.ANY)] * 11,
            ],
            out_specs=pl.BlockSpec((8, 32, 4, 384), lambda k, s, t: (0, 0, 0, 0)),
            scratch_shapes=[
                pltpu.VMEM((48 * PITCH, 128), F32),
                pltpu.VMEM((48 * PITCH, 128), F32),
                pltpu.VMEM((32 * 96, 128), F32),
                pltpu.VMEM((L // 8, 128, 128), BF),
                pltpu.VMEM((PAIR_DEV, 128, KPAD), BF),
                pltpu.SemaphoreType.DMA((32,)),
                pltpu.SemaphoreType.DMA((3,)),
            ],
        ),
        compiler_params=pltpu.CompilerParams(vmem_limit_bytes=56 * 2**20),
        name="cycle_sums",
    )(e, twist, coeffs, *gathered, *angular)


SOURCES_STEP = 16


def pixels_kernel(in_ref, basis_ref, dens_ref, disp_ref, total):
    step = pl.program_id(0)
    col = lax.broadcasted_iota(jnp.int32, (16, 96), 1)
    order = col % PAIR_DEV
    odd = (order + jnp.where(col >= 48, 1, 0)) % 2 == 1
    acc = None
    for source in range(SOURCES_STEP):
        value = in_ref[0, source].astype(F32)
        for radial in range(1, 8):
            value = value + in_ref[radial, source].astype(F32)
        value = jnp.concatenate([value[:, 96 * part : 96 * part + 96] for part in range(4)], axis=0)
        top = value.astype(BF).astype(F32)
        rest = value - top
        rows = jnp.concatenate(
            [
                jnp.where(odd, 0.0, top),
                jnp.where(odd, top, 0.0),
                jnp.where(odd, 0.0, rest),
                jnp.where(odd, rest, 0.0),
            ],
            axis=0,
        ).astype(BF)
        part = jnp.dot(rows, basis_ref[source], preferred_element_type=F32)
        part = part[0:32] + part[32:64]
        acc = part if acc is None else acc + part

    @pl.when(step == 0)
    def _():
        total[...] = acc

    @pl.when(step > 0)
    def _():
        total[...] += acc

    @pl.when(step == pl.num_programs(0) - 1)
    def _():
        even, odd_part = total[0:16], total[16:32]
        near, far = even + odd_part, even - odd_part
        for cycle in range(2):
            for shell in range(4):
                at = cycle * 8 + shell
                for ref, row in ((dens_ref, at), (disp_ref, at + 4)):
                    ref[shell, cycle : cycle + 1, 0:HALF_PIX] = near[row : row + 1]
                    ref[shell, cycle : cycle + 1, HALF_PIX:] = far[row : row + 1]


def pixel_basis():
    source = np.arange(32)[:, None, None]
    i = np.arange(PAIR_DEV)[None, None, :]
    low = PAIR_DEV * source + i
    orders = np.concatenate([low, L - 1 - low], axis=1)
    phase = (orders[..., None] * (np.arange(HALF_PIX) + 1)) % 2048
    angle = 2.0 * math.pi / 2048 * phase
    basis = np.stack([np.cos(angle), -np.sin(angle)], axis=2)
    return basis.reshape(32, 96, HALF_PIX).astype(jnp.bfloat16)


def pixels(received):
    out = jax.ShapeDtypeStruct((4, 2, 2 * HALF_PIX), F32)
    spec = pl.BlockSpec((4, 2, 2 * HALF_PIX), lambda k: (0, 0, 0))
    return pl.pallas_call(
        pixels_kernel,
        out_shape=(out, out),
        grid=(32 // SOURCES_STEP,),
        in_specs=[
            pl.BlockSpec((8, SOURCES_STEP, 4, 384), lambda k: (0, k, 0, 0)),
            pl.BlockSpec((SOURCES_STEP, 96, HALF_PIX), lambda k: (k, 0, 0)),
        ],
        out_specs=(spec, spec),
        scratch_shapes=[pltpu.VMEM((32, HALF_PIX), F32)],
        compiler_params=pltpu.CompilerParams(vmem_limit_bytes=48 * 2**20),
        name="pixels",
    )(received, jnp.asarray(pixel_basis()))


def table_kernel(r_ref, bessel_ref, counts_ref, out_ref, stage, grouped):
    width = bessel_ref.shape[3]
    mode = lax.broadcasted_iota(jnp.int32, (MODES_DEV, width), 0) + MODES_DEV * r_ref[0]
    live = mode < counts_ref[...]
    lane = lax.broadcasted_iota(jnp.int32, (8, 128), 1)
    for owner in range(8):
        for f in range(2):
            for shell in range(4):
                row = (f * 32 + owner * 4 + shell) * ROW_PITCH
                value = bessel_ref[f, owner * 4 + shell].astype(F32)
                stage[row : row + MODES_DEV, 0:width] = jnp.where(live, value, 0.0)

    def one(owner, carry):
        parts = [
            stage[pl.ds(owner * 8 * ROW_PITCH + n, 8, stride=ROW_PITCH), :] for n in range(MODES_DEV)
        ]
        parts = exchange([pltpu.roll(x, 4 * n, 1) if n else x for n, x in enumerate(parts)], lane)
        for g in range(width // 4):
            grouped[g, pl.ds(pl.multiple_of(owner * 8, 8), 8), :] = parts[g]
        return carry

    lax.fori_loop(0, 8, one, 0, unroll=2)
    for g in range(width // 8):
        turned = [jnp.transpose(grouped[2 * g + d]) for d in range(2)]
        out_ref[g] = jnp.concatenate(turned, axis=1).astype(BF)


def radial_table(bessel, mode_counts):
    width = bessel.shape[3]
    counts = lax.dynamic_slice_in_dim(mode_counts, lax.axis_index("ell") * width, width)
    return pl.pallas_call(
        table_kernel,
        out_shape=jax.ShapeDtypeStruct((width // 8, 128, 128), BF),
        grid_spec=pltpu.PrefetchScalarGridSpec(
            num_scalar_prefetch=1,
            grid=(1,),
            in_specs=[
                pl.BlockSpec(bessel.shape, lambda k, s: (0, 0, 0, 0)),
                pl.BlockSpec((1, width), lambda k, s: (0, 0)),
            ],
            out_specs=pl.BlockSpec((width // 8, 128, 128), lambda k, s: (0, 0, 0)),
            scratch_shapes=[
                pltpu.VMEM((64 * ROW_PITCH, 128), F32),
                pltpu.VMEM((width // 4, 64, 128), F32),
            ],
        ),
        compiler_params=pltpu.CompilerParams(vmem_limit_bytes=32 * 2**20),
        name="radial_table",
    )(lax.axis_index("rad").reshape(1).astype(jnp.int32), bessel, counts.reshape(1, width))


def ring_shift(value, shift, first):
    pairs = []
    for e in range(32):
        core, x, y = e % 2, (e // 2) % 4, e // 8
        if (core == 0) == first:
            x = (x + shift) % 4
        else:
            y = (y + shift) % 4
        pairs.append((e, (y * 4 + x) * 2 + core))
    return lax.ppermute(value, "ell", pairs)


def other_core(value):
    return lax.ppermute(value, "ell", [(e, e ^ 1) for e in range(32)])


def twist_table():
    low = np.arange(L // 2).reshape(32, PAIR_DEV)
    orders = np.concatenate([low, L - 1 - low], axis=1)
    weight = np.where(orders == 0, 1.0, 2.0)
    angle = 2.0 * math.pi / 4096 * orders
    return np.stack([weight * np.cos(angle), weight * np.sin(angle), weight], axis=1).reshape(96, 48).astype(np.float32)


def local(coefficients, legendre, bessel, mode_counts):
    e = lax.axis_index("ell")
    e_arr = e.reshape(1).astype(jnp.int32)
    twist = jnp.asarray(twist_table())
    table = radial_table(bessel, mode_counts)
    moved = [ring_shift(table, shift, True) for shift in SHIFTS[1:]]
    early = angular_blocks(e_arr, legendre, *ANGULAR_PARTS[0])
    early, *moved = lax.optimization_barrier((early, *moved))
    own = jnp.concatenate([table, *moved], axis=0)
    far = [ring_shift(own, shift, False) for shift in SHIFTS[1:]]
    e_late, own = lax.optimization_barrier((e_arr, own))
    coeffs = coeff_blocks(e_late, coefficients)
    middle = angular_blocks(e_late, legendre, *ANGULAR_PARTS[1])
    coeffs, middle, *far = lax.optimization_barrier((coeffs, middle, *far))
    mine = [own, *far]
    theirs = [other_core(value) for value in mine]
    e_last, *far = lax.optimization_barrier((e_arr, *far))
    late = angular_blocks(e_last, legendre, *ANGULAR_PARTS[2])
    late, *theirs = lax.optimization_barrier((late, *theirs))
    gathered = mine + theirs
    angular = (early, middle, late)
    sums = cycle_sums(e_arr, twist, coeffs, gathered, angular)
    received = lax.all_to_all(
        sums.reshape(256, 4, 384), ("rad", "ell"), split_axis=0, concat_axis=0, tiled=True
    )
    return pixels(received.reshape(8, 32, 4, 384))


def solution(mesh):
    in_specs = (P(None, "rad", "ell", None), P(None, "ell", None), P(None, None, "rad", "ell"), P())
    out_specs = (P("rad", "ell", None), P("rad", "ell", None))
    return jax.shard_map(local, mesh=mesh, in_specs=in_specs, out_specs=out_specs, check_vma=False)
```
